32 devices in a mesh: tgt: 4 (over y, x), src: 8 (over z, core).
Axes of the slice: x: 2, y: 2, z: 4, core: 2. Of those that a mesh axis runs over, the one named last changes fastest.
Arguments:
- positions: float32 [3, 8192], P(None, ('tgt', 'src')), may hold values from -6 to 6
- forces: float32 [3, 8192], P(None, ('tgt', 'src')), may hold values from -6 to 6
- neighbours: int32 [12, 8192], P(None, ('tgt', 'src')), may hold values from 0 to 255
- patch_owner: int32 [8192, 1], P(('tgt', 'src')), may hold values from 0 to 31; in each aligned block of 256 rows (0 to 255, 256 to 511, ...) at most 40 rows name the same one
- rest_length: float32 [6, 40960], P(None, ('tgt', 'src')), may hold values from 1 to 4
- moduli: float32 [2, 40960], P(None, ('tgt', 'src')), may hold values from 0.1 to 1
- rest_bend: float32 [3, 40960], P(None, ('tgt', 'src')), may hold values from -3 to 3
Outputs:
- final_positions: float32 [3, 8192], P(None, ('tgt', 'src'))
- final_velocity: float32 [3, 8192], P(None, ('tgt', 'src'))
The draws below stay inside these ranges and needn't reach their ends.
Inputs may be any that keep to these rules, and one draw needn't show every extreme that they name: patch_owner[n, 0] is a flattened device index, tgt slowest; within the 256 nodes of one device no owner is named more than 40 times, and some device names some owner exactly 40 times. `neighbours`: indices into the node's own block of 256 nodes.
All inputs are finite; a program needn't handle non-finite values.
Results may differ from the reference program's by a relative error of at most 0.0003.
Values sent between devices are 32-bit elements; how exact they have to be, the bound alone decides.
No kernel may reach another device: no remote copies, remote signals or barrier semaphores. Data moves between devices by JAX's collectives and lax.ppermute only.
A program may use at most 64 MiB of HBM per device.

```python
import math
import jax
import jax.numpy as jnp
import numpy as np
from jax import lax

NODES_DEV = 256
STEPS = 3
CYCLE = 12
NODES = 8192
CAP = 40
ALL_SLOTS = 40960
N_TGT = 4
N_SRC = 8
DEVICES = 32


def touch_ends(drawn, stream_key, smallest, largest):
    dims = drawn.shape
    index_at = [jax.random.randint(jax.random.fold_in(stream_key, axis), (), 0, dims[axis]) for axis in range(len(dims))]
    drawn = drawn.at[tuple(index_at)].set(smallest)
    longest = dims.index(max(dims))
    index_at[longest] = (index_at[longest] + 1) % dims[longest]
    return drawn.at[tuple(index_at)].set(largest)


def shard_levels(stream_key, extent, cuts, low, largest):
    def one(axis_at, shards_of):
        heights = jax.random.uniform(jax.random.fold_in(jax.random.fold_in(stream_key, 6), axis_at), (shards_of,), jnp.float32, low / len(cuts), largest / len(cuts))
        return jnp.repeat(jnp.exp(heights), extent[axis_at] // shards_of).reshape((-1,) + (1,) * (len(extent) - axis_at - 1))

    gain = one(*cuts[0])
    for cut in cuts[1:]:
        gain = gain * one(*cut)
    return gain


def routed_block(key, own, number, rows, amount, top, most, skew):
    ranking = jax.random.permutation(key, amount)
    heavy_load, common = load_shares(amount, rows * top, most, skew, True), load_shares(amount, rows * top, most, skew, False)
    places = jnp.arange(amount)

    def named(tallies, offset_by):
        used = int((tallies > 0).sum())
        fixed = max(1, used // 4)
        passed = fixed + (places - fixed + offset_by * (used - fixed)) % max(1, amount - fixed)
        return jnp.zeros((amount,), jnp.int32).at[ranking[jnp.where(places < fixed, places, passed)]].set(jnp.asarray(tallies, jnp.int32))

    tallies = jnp.where(number % 4 == 0, named(heavy_load, number // 4), named(common, number - number // 4 - 1))
    mixed = jax.random.permutation(jax.random.fold_in(own, 3), amount)
    giver, taker = mixed[0:amount // 2 * 2:2], mixed[1:amount // 2 * 2:2]
    slack = jnp.minimum(tallies[giver] - 1, most - tallies[taker]) // 2
    slack = jnp.where((giver == ranking[0]) | (taker == ranking[0]) | (tallies[taker] == 0), 0, jnp.maximum(slack, 0))
    passed = jax.random.randint(jax.random.fold_in(own, 4), (amount // 2,), 0, 1 << 20) % (slack + 1)
    tallies = tallies.at[giver].add(-passed).at[taker].add(passed)
    items = jnp.searchsorted(jnp.cumsum(tallies), jnp.arange(rows * top), side="right").astype(jnp.int32)
    grid = items.reshape(top, rows).T
    grid = grid[jax.random.permutation(jax.random.fold_in(own, 1), rows)]
    offset_by = jax.random.randint(jax.random.fold_in(own, 2), (rows, 1), 0, top)
    return jnp.take_along_axis(grid, (jnp.arange(top)[None, :] + offset_by) % top, axis=1)


def load_shares(count, total, reach, skew, full):
    portions = [(1 << 20) // math.isqrt(standing ** skew) + 1 for standing in range(1, count + 1)]
    largest = reach if full else min(reach, max(-(-total // count), total * portions[0] // sum(portions)))
    least = 1 if total - largest >= count - 1 else 0
    counts, rest = [largest] + [least] * (count - 1), total - largest - least * (count - 1)
    while rest > 0:
        movable = [i for i in range(1, count) if counts[i] < largest] or [i for i in range(1, count) if counts[i] < reach]
        mass, left = sum([portions[i] for i in movable]), rest
        for i in movable:
            more = min(reach - counts[i], max(1, left * portions[i] // mass), rest)
            counts[i] = counts[i] + more
            rest = rest - more
    return np.array(counts)


def normal_values(key, dims, scale, limit, pieces=(), kind=jnp.bfloat16):
    loudness = shard_levels(key, dims, pieces, -0.22, 0.18) if pieces else 1.0
    values = jax.random.normal(key, dims, jnp.float32) * scale * loudness
    return jnp.minimum(jnp.maximum(values, -limit), limit).astype(kind)


def setup_inputs(seed: int = 0) -> dict:
    seeds = jax.random.split(jax.random.key(seed), 8)
    positions = normal_values(seeds[0], (3, NODES), 1.0, 6.0, ((1, 32),), jnp.float32)
    forces = normal_values(seeds[1], (3, NODES), 1.0, 6.0, ((1, 32),), jnp.float32)
    neighbours = touch_ends(jax.random.randint(seeds[2], (CYCLE, NODES), 0, NODES_DEV), jax.random.fold_in(seeds[2], 1), 0, NODES_DEV - 1).astype(jnp.int32)
    patch_owner_keys = jax.random.split(jax.random.fold_in(seeds[3], 1), NODES // NODES_DEV)
    patch_owner_turns = jax.random.permutation(jax.random.fold_in(seeds[3], 3), NODES // NODES_DEV)
    patch_owner = jax.vmap(lambda own, number: routed_block(jax.random.fold_in(seeds[3], 2), own, number, NODES_DEV, DEVICES, 1, CAP, 2))(patch_owner_keys, patch_owner_turns).reshape((NODES, 1))
    rest_length = jnp.clip(jnp.exp(math.log(4.0) - 1.3862944 * jax.random.uniform(seeds[4], (6, ALL_SLOTS), jnp.float32) ** shard_levels(seeds[4], (6, ALL_SLOTS), ((1, 32),), -0.2, 0.2)), 1.0, 4.0)
    moduli = jnp.clip(jnp.exp(math.log(1.0) - 2.3025851 * jax.random.uniform(seeds[5], (2, ALL_SLOTS), jnp.float32) ** shard_levels(seeds[5], (2, ALL_SLOTS), ((1, 32),), -0.2, 0.2)), 0.1, 1.0)
    rest_bend = normal_values(seeds[6], (3, ALL_SLOTS), 0.5, 3.0, ((1, 32),), jnp.float32)
    return dict(positions=positions, forces=forces, neighbours=neighbours, patch_owner=patch_owner, rest_length=rest_length, moduli=moduli, rest_bend=rest_bend)


blob_square = 0.0025
time_step = 0.5

def pick_block(length, wanted):
    return wanted if length % wanted == 0 else length

def stokes_block(target_pos, source_pos, source_force):
    delta = target_pos[:, :, None] - source_pos[:, None, :]
    radius_sq = lax.optimization_barrier(jnp.sum(delta * delta, axis=0))
    shifted = radius_sq + blob_square
    inverse = 1.0 / (shifted * jnp.sqrt(shifted))
    along = lax.optimization_barrier(jnp.sum(delta * source_force[:, None, :], axis=0))
    direct = (radius_sq + 2.0 * blob_square) * inverse
    tensor = along * inverse
    return lax.optimization_barrier(jnp.sum(direct[None] * source_force[:, None, :] + tensor[None] * delta, axis=2))

def stokes_sum(target_pos, source_pos, source_force):
    count_target = target_pos.shape[1]
    count_source = source_pos.shape[1]
    target_rows = pick_block(count_target, 512)
    source_rows = pick_block(count_source, 2048)
    targets = target_pos.reshape(3, count_target // target_rows, target_rows).transpose(1, 0, 2)
    sources = source_pos.reshape(3, count_source // source_rows, source_rows).transpose(1, 0, 2)
    weights = source_force.reshape(3, count_source // source_rows, source_rows).transpose(1, 0, 2)

    def per_target(target_block):

        def add_block(running, blocks):
            return (running + stokes_block(target_block, blocks[0], blocks[1]), None)
        total, _ = lax.scan(add_block, jnp.zeros((3, target_rows), jnp.float32), (sources, weights))
        return total
    result = lax.map(per_target, targets)
    return result.transpose(1, 0, 2).reshape(3, count_target)

def cycle_weights():
    return jnp.concatenate([jnp.full((6,), 2.0 / 9.0, jnp.float32), jnp.full((6,), -1.0 / 18.0, jnp.float32)])

def membrane_force(edges, rest_length, moduli, rest_bend):
    nearest = edges[:, :6, :]
    stretch = lax.optimization_barrier(jnp.sum(nearest * nearest, axis=0)) / (rest_length * rest_length)
    tension = (stretch - 1.0) / (stretch + 1.0)
    surface = moduli[0] * lax.optimization_barrier(jnp.sum((tension / rest_length)[None] * nearest, axis=1))
    bending = lax.optimization_barrier(jnp.sum(cycle_weights()[None, :, None] * edges, axis=1)) - rest_bend
    return surface + moduli[1] * bending

def reference(positions, forces, neighbours, patch_owner, rest_length, moduli, rest_bend):
    devices = N_TGT * N_SRC
    total_nodes = positions.shape[1]
    owners = patch_owner[:, 0].reshape(devices, NODES_DEV)
    onehot = (owners[:, :, None] == jnp.arange(devices, dtype=jnp.int32)[None, None, :]).astype(jnp.int32)
    before = jnp.cumsum(onehot, axis=1) - onehot
    rank = lax.optimization_barrier(jnp.sum(before * onehot, axis=2))
    column = (owners * (devices * CAP) + jnp.arange(devices, dtype=jnp.int32)[:, None] * CAP + rank).reshape(total_nodes)
    node_length = rest_length[:, column]
    node_moduli = moduli[:, column]
    node_bend = rest_bend[:, column]
    base = jnp.arange(total_nodes, dtype=jnp.int32) // NODES_DEV * NODES_DEV
    stencil = neighbours + base[None, :]
    scale = 1.0 / math.sqrt(total_nodes)
    current = positions
    load = forces
    for update in range(STEPS):
        velocity = stokes_sum(current, current, load) * scale
        current = current + time_step * velocity
        edges = current[:, stencil] - current[:, None, :]
        load = membrane_force(edges, node_length, node_moduli, node_bend)
    velocity = stokes_sum(current, current, load) * scale
    return (current, velocity)
```

```python
import functools
import math

import jax
import jax.numpy as jnp
from jax import lax
from jax.experimental import pallas as pl
from jax.experimental.pallas import tpu as pltpu
from jax.sharding import PartitionSpec as P

STEPS = 3
LANES = 128
ROWS = 8
TARGET_ROWS = 32
PARAMS = 16

blob_square = 0.0025
time_step = 0.5

AXES = ("tgt", "src")
VMEM = pl.BlockSpec(memory_space=pltpu.VMEM)
GRANT = pltpu.CompilerParams(vmem_limit_bytes=32 * 1024 * 1024)


def pack_kernel(length_ref, moduli_ref, bend_ref, out_ref):
    devices, _, capacity = out_ref.shape
    for device in range(devices):
        cut = slice(device * capacity, (device + 1) * capacity)
        out_ref[device, 0:6, :] = length_ref[:, cut]
        out_ref[device, 6:8, :] = moduli_ref[:, cut]
        out_ref[device, 8:11, :] = bend_ref[:, cut]
        out_ref[device, 11:PARAMS, :] = jnp.zeros((PARAMS - 11, capacity), jnp.float32)


def pack_slots(rest_length, moduli, rest_bend, devices):
    capacity = rest_length.shape[1] // devices
    return pl.pallas_call(
        pack_kernel,
        out_shape=jax.ShapeDtypeStruct((devices, PARAMS, capacity), jnp.float32),
        in_specs=[VMEM] * 3,
        out_specs=VMEM,
        compiler_params=GRANT,
    )(rest_length, moduli, rest_bend)


def pick_kernel(slots_ref, owner_ref, out_ref):
    devices, _, capacity = slots_ref.shape
    nodes = owner_ref.shape[1]
    owner = owner_ref[...]
    across = jnp.broadcast_to(owner, (nodes, nodes))
    down = across.T
    earlier = lax.broadcasted_iota(jnp.int32, (nodes, nodes), 0) < lax.broadcasted_iota(
        jnp.int32, (nodes, nodes), 1
    )
    rank = jnp.sum(jnp.where((across == down) & earlier, 1, 0), axis=0, keepdims=True)
    for at in range(0, nodes, LANES):
        place = jnp.broadcast_to(rank[:, at : at + LANES], (ROWS, LANES))
        named = jnp.broadcast_to(owner[:, at : at + LANES], (ROWS, LANES))
        for row in range(0, PARAMS, ROWS):

            def choose(device, chosen):
                block = slots_ref[device, row : row + ROWS, :]
                block = jnp.concatenate([block, jnp.zeros((ROWS, LANES - capacity), jnp.float32)], axis=1)
                taken = jnp.take_along_axis(block, place, axis=1, mode="promise_in_bounds")
                return jnp.where(named == device, taken, chosen)

            out_ref[row : row + ROWS, at : at + LANES] = lax.fori_loop(
                0, devices, choose, jnp.zeros((ROWS, LANES), jnp.float32), unroll=4
            )


def pick_slots(slots, owner):
    return pl.pallas_call(
        pick_kernel,
        out_shape=jax.ShapeDtypeStruct((PARAMS, owner.shape[1]), jnp.float32),
        in_specs=[VMEM] * 2,
        out_specs=VMEM,
        compiler_params=GRANT,
    )(slots, owner)


def pair_sums(all_ref, own_ref, column_ref, sum_ref):
    devices, _, nodes = all_ref.shape
    for c in range(3):
        for at in range(0, nodes, LANES):
            row = own_ref[c : c + 1, at : at + LANES]
            column_ref[c, at : at + LANES, :] = jnp.broadcast_to(row, (LANES, LANES)).T

    def per_target(block, _):
        rows = pl.ds(pl.multiple_of(block * TARGET_ROWS, TARGET_ROWS), TARGET_ROWS)
        target = [column_ref[c, rows, :] for c in range(3)]

        def per_source(device, totals):
            for at in range(0, nodes, LANES):
                x = [all_ref[device, c : c + 1, at : at + LANES] for c in range(3)]
                f = [all_ref[device, 3 + c : 4 + c, at : at + LANES] for c in range(3)]
                d = [target[c] - x[c] for c in range(3)]
                shifted = d[0] * d[0] + (d[1] * d[1] + (d[2] * d[2] + blob_square))
                r = lax.rsqrt(shifted)
                cube = r * (r * r)
                direct = r + blob_square * cube
                along = (d[0] * f[0] + d[1] * f[1] + d[2] * f[2]) * cube
                totals = tuple(totals[c] + (direct * f[c] + along * d[c]) for c in range(3))
            return totals

        zero = jnp.zeros((TARGET_ROWS, LANES), jnp.float32)
        totals = lax.fori_loop(0, devices, per_source, (zero, zero, zero), unroll=2)
        for c in range(3):
            sum_ref[c, rows, :] = totals[c]
        return 0

    lax.fori_loop(0, nodes // TARGET_ROWS, per_target, 0)
    scale = 1.0 / math.sqrt(devices * nodes)
    velocity = []
    for c in range(3):
        parts = [
            jnp.sum(sum_ref[c, at : at + LANES, :].T, axis=0, keepdims=True)
            for at in range(0, nodes, LANES)
        ]
        velocity.append(jnp.concatenate(parts, axis=1) * scale)
    return velocity


def membrane(x, neighbours_ref, params_ref):
    nodes = x[0].shape[1]
    force = [[], [], []]
    for at in range(0, nodes, LANES):
        here = slice(at, at + LANES)
        points = [neighbours_ref[0:6, here], neighbours_ref[6:12, here]]
        edges = []
        for index in points:
            local = index & (LANES - 1)
            group = index // LANES
            component = []
            for c in range(3):
                found = jnp.zeros(index.shape, jnp.float32)
                for part in range(nodes // LANES):
                    source = jnp.broadcast_to(x[c][:, part * LANES : (part + 1) * LANES], index.shape)
                    taken = jnp.take_along_axis(source, local, axis=1, mode="promise_in_bounds")
                    found = jnp.where(group == part, taken, found)
                component.append(found - x[c][:, here])
            edges.append(component)
        near, far = edges
        length = params_ref[0:6, here]
        stretch = (near[0] * near[0] + near[1] * near[1] + near[2] * near[2]) / (length * length)
        tension = (stretch - 1.0) / (stretch + 1.0) / length
        for c in range(3):
            surface = jnp.sum(tension * near[c], axis=0, keepdims=True)
            bending = jnp.sum((2.0 / 9.0) * near[c] - (1.0 / 18.0) * far[c], axis=0, keepdims=True)
            bending = bending - params_ref[8 + c : 9 + c, here]
            force[c].append(params_ref[6:7, here] * surface + params_ref[7:8, here] * bending)
    return [jnp.concatenate(parts, axis=1) for parts in force]


def step_kernel(all_ref, own_ref, neighbours_ref, params_ref, out_ref, column_ref, sum_ref):
    velocity = pair_sums(all_ref, own_ref, column_ref, sum_ref)
    x = [own_ref[c : c + 1, :] + time_step * velocity[c] for c in range(3)]
    force = membrane(x, neighbours_ref, params_ref)
    for c in range(3):
        out_ref[c : c + 1, :] = x[c]
        out_ref[3 + c : 4 + c, :] = force[c]
    out_ref[6:ROWS, :] = jnp.zeros((ROWS - 6, x[0].shape[1]), jnp.float32)


def last_kernel(all_ref, own_ref, position_ref, velocity_ref, column_ref, sum_ref):
    velocity = pair_sums(all_ref, own_ref, column_ref, sum_ref)
    position_ref[...] = own_ref[0:3, :]
    for c in range(3):
        velocity_ref[c : c + 1, :] = velocity[c]


def scratch(nodes):
    return [pltpu.VMEM((3, nodes, LANES), jnp.float32), pltpu.VMEM((3, nodes, LANES), jnp.float32)]


def gather_state(state):
    return lax.all_gather(state, AXES, axis=0)


def body(positions, forces, neighbours, patch_owner, rest_length, moduli, rest_bend):
    devices = lax.axis_size("tgt") * lax.axis_size("src")
    nodes = positions.shape[1]
    slots = lax.all_to_all(
        pack_slots(rest_length, moduli, rest_bend, devices), AXES, split_axis=0, concat_axis=0, tiled=True
    )
    state = jnp.concatenate([positions, forces, jnp.zeros((ROWS - 6, nodes), jnp.float32)], axis=0)
    params = pick_slots(slots, patch_owner.reshape(1, nodes))
    for _ in range(STEPS):
        state = pl.pallas_call(
            step_kernel,
            out_shape=jax.ShapeDtypeStruct((ROWS, nodes), jnp.float32),
            in_specs=[VMEM] * 4,
            out_specs=VMEM,
            scratch_shapes=scratch(nodes),
            compiler_params=GRANT,
        )(gather_state(state), state, neighbours, params)
    return pl.pallas_call(
        last_kernel,
        out_shape=(jax.ShapeDtypeStruct((3, nodes), jnp.float32),) * 2,
        in_specs=[VMEM] * 2,
        out_specs=(VMEM,) * 2,
        scratch_shapes=scratch(nodes),
        compiler_params=GRANT,
    )(gather_state(state), state)


def solution(mesh):
    placed = (
        P(None, AXES),
        P(None, AXES),
        P(None, AXES),
        P(AXES, None),
        P(None, AXES),
        P(None, AXES),
        P(None, AXES),
    )
    return jax.shard_map(
        body,
        mesh=mesh,
        in_specs=placed,
        out_specs=(P(None, AXES), P(None, AXES)),
        check_vma=False,
    )
```

```python
import functools
import math

import jax
import jax.numpy as jnp
from jax import lax
from jax.experimental import pallas as pl
from jax.experimental.pallas import tpu as pltpu
from jax.sharding import PartitionSpec as P

STEPS = 3
LANES = 128
ROWS = 8
TARGET_ROWS = 32
PARAMS = 16

blob_square = 0.0025
time_step = 0.5

AXES = ("tgt", "src")
VMEM = pl.BlockSpec(memory_space=pltpu.VMEM)
GRANT = pltpu.CompilerParams(vmem_limit_bytes=32 * 1024 * 1024)


def pack_kernel(length_ref, moduli_ref, bend_ref, out_ref):
    devices = out_ref.shape[0]
    capacity = length_ref.shape[1] // devices
    out_ref[...] = jnp.zeros(out_ref.shape, jnp.float32)
    for device in range(devices):
        cut = slice(device * capacity, (device + 1) * capacity)
        out_ref[device, 0:6, 0:capacity] = length_ref[:, cut]
        out_ref[device, 6:8, 0:capacity] = moduli_ref[:, cut]
        out_ref[device, 0:3, capacity : 2 * capacity] = bend_ref[:, cut]


def pack_slots(rest_length, moduli, rest_bend, devices):
    return pl.pallas_call(
        pack_kernel,
        out_shape=jax.ShapeDtypeStruct((devices, ROWS, LANES), jnp.float32),
        in_specs=[VMEM] * 3,
        out_specs=VMEM,
        compiler_params=GRANT,
    )(rest_length, moduli, rest_bend)


def pick_kernel(capacity, slots_ref, owner_ref, out_ref):
    devices = slots_ref.shape[0]
    nodes = owner_ref.shape[1]
    owner = owner_ref[...]
    across = jnp.broadcast_to(owner, (nodes, nodes))
    down = across.T
    earlier = lax.broadcasted_iota(jnp.int32, (nodes, nodes), 0) < lax.broadcasted_iota(
        jnp.int32, (nodes, nodes), 1
    )
    rank = jnp.sum(jnp.where((across == down) & earlier, 1, 0), axis=0, keepdims=True)
    for at in range(0, nodes, LANES):
        place = jnp.broadcast_to(rank[:, at : at + LANES], (ROWS, LANES))
        named = jnp.broadcast_to(owner[:, at : at + LANES], (ROWS, LANES))
        for part in range(PARAMS // ROWS):

            def choose(device, chosen):
                taken = jnp.take_along_axis(
                    slots_ref[device], place + part * capacity, axis=1, mode="promise_in_bounds"
                )
                return jnp.where(named == device, taken, chosen)

            out_ref[part * ROWS : (part + 1) * ROWS, at : at + LANES] = lax.fori_loop(
                0, devices, choose, jnp.zeros((ROWS, LANES), jnp.float32), unroll=4
            )


def pick_slots(slots, owner, capacity):
    return pl.pallas_call(
        functools.partial(pick_kernel, capacity),
        out_shape=jax.ShapeDtypeStruct((PARAMS, owner.shape[1]), jnp.float32),
        in_specs=[VMEM] * 2,
        out_specs=VMEM,
        compiler_params=GRANT,
    )(slots, owner)


def pair_sums(all_ref, own_ref, column_ref, sum_ref):
    devices, _, nodes = all_ref.shape
    for c in range(3):
        for at in range(0, nodes, LANES):
            row = own_ref[c : c + 1, at : at + LANES]
            column_ref[c, at : at + LANES, :] = jnp.broadcast_to(row, (LANES, LANES)).T

    def per_target(block, _):
        rows = pl.ds(pl.multiple_of(block * TARGET_ROWS, TARGET_ROWS), TARGET_ROWS)
        target = [column_ref[c, rows, :] for c in range(3)]

        def per_source(device, totals):
            for at in range(0, nodes, LANES):
                x = [all_ref[device, c : c + 1, at : at + LANES] for c in range(3)]
                f = [all_ref[device, 3 + c : 4 + c, at : at + LANES] for c in range(3)]
                d = [target[c] - x[c] for c in range(3)]
                shifted = d[0] * d[0] + (d[1] * d[1] + (d[2] * d[2] + blob_square))
                r = lax.rsqrt(shifted)
                cube = r * (r * r)
                direct = r + blob_square * cube
                along = (d[0] * f[0] + d[1] * f[1] + d[2] * f[2]) * cube
                totals = tuple(totals[c] + (direct * f[c] + along * d[c]) for c in range(3))
            return totals

        zero = jnp.zeros((TARGET_ROWS, LANES), jnp.float32)
        totals = lax.fori_loop(0, devices, per_source, (zero, zero, zero), unroll=2)
        for c in range(3):
            sum_ref[c, rows, :] = totals[c]
        return 0

    lax.fori_loop(0, nodes // TARGET_ROWS, per_target, 0)
    scale = 1.0 / math.sqrt(devices * nodes)
    velocity = []
    for c in range(3):
        parts = [
            jnp.sum(sum_ref[c, at : at + LANES, :].T, axis=0, keepdims=True)
            for at in range(0, nodes, LANES)
        ]
        velocity.append(jnp.concatenate(parts, axis=1) * scale)
    return velocity


def membrane(x, neighbours_ref, params_ref):
    nodes = x[0].shape[1]
    force = [[], [], []]
    for at in range(0, nodes, LANES):
        here = slice(at, at + LANES)
        points = [neighbours_ref[0:6, here], neighbours_ref[6:12, here]]
        edges = []
        for index in points:
            local = index & (LANES - 1)
            group = index // LANES
            component = []
            for c in range(3):
                found = jnp.zeros(index.shape, jnp.float32)
                for part in range(nodes // LANES):
                    source = jnp.broadcast_to(x[c][:, part * LANES : (part + 1) * LANES], index.shape)
                    taken = jnp.take_along_axis(source, local, axis=1, mode="promise_in_bounds")
                    found = jnp.where(group == part, taken, found)
                component.append(found - x[c][:, here])
            edges.append(component)
        near, far = edges
        length = params_ref[0:6, here]
        stretch = (near[0] * near[0] + near[1] * near[1] + near[2] * near[2]) / (length * length)
        tension = (stretch - 1.0) / (stretch + 1.0) / length
        for c in range(3):
            surface = jnp.sum(tension * near[c], axis=0, keepdims=True)
            bending = jnp.sum((2.0 / 9.0) * near[c] - (1.0 / 18.0) * far[c], axis=0, keepdims=True)
            bending = bending - params_ref[8 + c : 9 + c, here]
            force[c].append(params_ref[6:7, here] * surface + params_ref[7:8, here] * bending)
    return [jnp.concatenate(parts, axis=1) for parts in force]


def step_kernel(all_ref, own_ref, neighbours_ref, params_ref, out_ref, column_ref, sum_ref):
    velocity = pair_sums(all_ref, own_ref, column_ref, sum_ref)
    x = [own_ref[c : c + 1, :] + time_step * velocity[c] for c in range(3)]
    force = membrane(x, neighbours_ref, params_ref)
    for c in range(3):
        out_ref[c : c + 1, :] = x[c]
        out_ref[3 + c : 4 + c, :] = force[c]
    out_ref[6:ROWS, :] = jnp.zeros((ROWS - 6, x[0].shape[1]), jnp.float32)


def last_kernel(all_ref, own_ref, position_ref, velocity_ref, column_ref, sum_ref):
    velocity = pair_sums(all_ref, own_ref, column_ref, sum_ref)
    position_ref[...] = own_ref[0:3, :]
    for c in range(3):
        velocity_ref[c : c + 1, :] = velocity[c]


def scratch(nodes):
    return [pltpu.VMEM((3, nodes, LANES), jnp.float32), pltpu.VMEM((3, nodes, LANES), jnp.float32)]


def gather_state(state, devices):
    spread = jnp.broadcast_to(state[None], (devices,) + state.shape)
    return lax.all_to_all(spread, AXES, split_axis=0, concat_axis=0, tiled=True)


def body(positions, forces, neighbours, patch_owner, rest_length, moduli, rest_bend):
    devices = lax.axis_size("tgt") * lax.axis_size("src")
    nodes = positions.shape[1]
    slots = lax.all_to_all(
        pack_slots(rest_length, moduli, rest_bend, devices), AXES, split_axis=0, concat_axis=0, tiled=True
    )
    state = jnp.concatenate([positions, forces, jnp.zeros((ROWS - 6, nodes), jnp.float32)], axis=0)
    params = pick_slots(slots, patch_owner.reshape(1, nodes), rest_length.shape[1] // devices)
    for _ in range(STEPS):
        state = pl.pallas_call(
            step_kernel,
            out_shape=jax.ShapeDtypeStruct((ROWS, nodes), jnp.float32),
            in_specs=[VMEM] * 4,
            out_specs=VMEM,
            scratch_shapes=scratch(nodes),
            compiler_params=GRANT,
        )(gather_state(state, devices), state, neighbours, params)
    return pl.pallas_call(
        last_kernel,
        out_shape=(jax.ShapeDtypeStruct((3, nodes), jnp.float32),) * 2,
        in_specs=[VMEM] * 2,
        out_specs=(VMEM,) * 2,
        scratch_shapes=scratch(nodes),
        compiler_params=GRANT,
    )(gather_state(state, devices), state)


def solution(mesh):
    placed = (
        P(None, AXES),
        P(None, AXES),
        P(None, AXES),
        P(AXES, None),
        P(None, AXES),
        P(None, AXES),
        P(None, AXES),
    )
    return jax.shard_map(
        body,
        mesh=mesh,
        in_specs=placed,
        out_specs=(P(None, AXES), P(None, AXES)),
        check_vma=False,
    )
```

```python
import functools
import math

import jax
import jax.numpy as jnp
from jax import lax
from jax.experimental import pallas as pl
from jax.experimental.pallas import tpu as pltpu
from jax.sharding import PartitionSpec as P

STEPS = 3
LANES = 128
ROWS = 8
TARGET_ROWS = 32
PARAMS = 16

blob_square = 0.0025
time_step = 0.5

AXES = ("tgt", "src")
VMEM = pl.BlockSpec(memory_space=pltpu.VMEM)
GRANT = pltpu.CompilerParams(vmem_limit_bytes=32 * 1024 * 1024)


def pack_kernel(length_ref, moduli_ref, bend_ref, out_ref):
    devices = out_ref.shape[0]
    capacity = length_ref.shape[1] // devices
    out_ref[...] = jnp.zeros(out_ref.shape, jnp.float32)
    for device in range(devices):
        cut = slice(device * capacity, (device + 1) * capacity)
        out_ref[device, 0:6, 0:capacity] = length_ref[:, cut]
        out_ref[device, 6:8, 0:capacity] = moduli_ref[:, cut]
        out_ref[device, 0:3, capacity : 2 * capacity] = bend_ref[:, cut]


def pack_slots(rest_length, moduli, rest_bend, devices):
    return pl.pallas_call(
        pack_kernel,
        out_shape=jax.ShapeDtypeStruct((devices, ROWS, LANES), jnp.float32),
        in_specs=[VMEM] * 3,
        out_specs=VMEM,
        compiler_params=GRANT,
    )(rest_length, moduli, rest_bend)


def pick_kernel(capacity, slots_ref, owner_ref, out_ref):
    devices = slots_ref.shape[0]
    nodes = owner_ref.shape[1]
    owner = owner_ref[...]
    across = jnp.broadcast_to(owner, (nodes, nodes))
    down = across.T
    earlier = lax.broadcasted_iota(jnp.int32, (nodes, nodes), 0) < lax.broadcasted_iota(
        jnp.int32, (nodes, nodes), 1
    )
    rank = jnp.sum(jnp.where((across == down) & earlier, 1, 0), axis=0, keepdims=True)
    for at in range(0, nodes, LANES):
        place = jnp.broadcast_to(rank[:, at : at + LANES], (ROWS, LANES))
        named = jnp.broadcast_to(owner[:, at : at + LANES], (ROWS, LANES))
        for part in range(PARAMS // ROWS):

            def choose(device, chosen):
                taken = jnp.take_along_axis(
                    slots_ref[device], place + part * capacity, axis=1, mode="promise_in_bounds"
                )
                return jnp.where(named == device, taken, chosen)

            out_ref[part * ROWS : (part + 1) * ROWS, at : at + LANES] = lax.fori_loop(
                0, devices, choose, jnp.zeros((ROWS, LANES), jnp.float32), unroll=4
            )


def pick_slots(slots, owner, capacity):
    return pl.pallas_call(
        functools.partial(pick_kernel, capacity),
        out_shape=jax.ShapeDtypeStruct((PARAMS, owner.shape[1]), jnp.float32),
        in_specs=[VMEM] * 2,
        out_specs=VMEM,
        compiler_params=GRANT,
    )(slots, owner)


def spread_columns(own_ref, column_ref):
    for c in range(3):
        for at in range(0, own_ref.shape[1], LANES):
            row = own_ref[c : c + 1, at : at + LANES]
            column_ref[c, at : at + LANES, :] = jnp.broadcast_to(row, (LANES, LANES)).T


def pair_sums(source_refs, column_ref, start_ref, sum_ref):
    nodes = column_ref.shape[1]

    def per_target(block, _):
        rows = pl.ds(pl.multiple_of(block * TARGET_ROWS, TARGET_ROWS), TARGET_ROWS)
        target = [column_ref[c, rows, :] for c in range(3)]
        if start_ref is None:
            totals = (jnp.zeros((TARGET_ROWS, LANES), jnp.float32),) * 3
        else:
            totals = tuple(start_ref[c, rows, :] for c in range(3))
        for source_ref in source_refs:

            def per_source(device, totals):
                for at in range(0, nodes, LANES):
                    x = [source_ref[device, c : c + 1, at : at + LANES] for c in range(3)]
                    f = [source_ref[device, 3 + c : 4 + c, at : at + LANES] for c in range(3)]
                    d = [target[c] - x[c] for c in range(3)]
                    shifted = d[0] * d[0] + (d[1] * d[1] + (d[2] * d[2] + blob_square))
                    r = lax.rsqrt(shifted)
                    cube = r * (r * r)
                    direct = r + blob_square * cube
                    along = (d[0] * f[0] + d[1] * f[1] + d[2] * f[2]) * cube
                    totals = tuple(totals[c] + (direct * f[c] + along * d[c]) for c in range(3))
                return totals

            totals = lax.fori_loop(0, source_ref.shape[0], per_source, totals, unroll=2)
        for c in range(3):
            sum_ref[c, rows, :] = totals[c]
        return 0

    lax.fori_loop(0, nodes // TARGET_ROWS, per_target, 0)


def velocity_rows(sum_ref, scale):
    nodes = sum_ref.shape[1]
    velocity = []
    for c in range(3):
        parts = [
            jnp.sum(sum_ref[c, at : at + LANES, :].T, axis=0, keepdims=True)
            for at in range(0, nodes, LANES)
        ]
        velocity.append(jnp.concatenate(parts, axis=1) * scale)
    return velocity


def membrane(x, neighbours_ref, params_ref):
    nodes = x[0].shape[1]
    force = [[], [], []]
    for at in range(0, nodes, LANES):
        here = slice(at, at + LANES)
        points = [neighbours_ref[0:6, here], neighbours_ref[6:12, here]]
        edges = []
        for index in points:
            local = index & (LANES - 1)
            group = index // LANES
            component = []
            for c in range(3):
                found = jnp.zeros(index.shape, jnp.float32)
                for part in range(nodes // LANES):
                    source = jnp.broadcast_to(x[c][:, part * LANES : (part + 1) * LANES], index.shape)
                    taken = jnp.take_along_axis(source, local, axis=1, mode="promise_in_bounds")
                    found = jnp.where(group == part, taken, found)
                component.append(found - x[c][:, here])
            edges.append(component)
        near, far = edges
        length = params_ref[0:6, here]
        stretch = (near[0] * near[0] + near[1] * near[1] + near[2] * near[2]) / (length * length)
        tension = (stretch - 1.0) / (stretch + 1.0) / length
        for c in range(3):
            surface = jnp.sum(tension * near[c], axis=0, keepdims=True)
            bending = jnp.sum((2.0 / 9.0) * near[c] - (1.0 / 18.0) * far[c], axis=0, keepdims=True)
            bending = bending - params_ref[8 + c : 9 + c, here]
            force[c].append(params_ref[6:7, here] * surface + params_ref[7:8, here] * bending)
    return [jnp.concatenate(parts, axis=1) for parts in force]


def near_kernel(source_ref, own_ref, column_ref, sum_ref):
    spread_columns(own_ref, column_ref)
    pair_sums([source_ref], column_ref, None, sum_ref)


def step_kernel(others, scale, *refs):
    own_ref, column_ref, start_ref, neighbours_ref, params_ref, out_ref, sum_ref = refs[others:]
    pair_sums(refs[:others], column_ref, start_ref, sum_ref)
    velocity = velocity_rows(sum_ref, scale)
    x = [own_ref[c : c + 1, :] + time_step * velocity[c] for c in range(3)]
    force = membrane(x, neighbours_ref, params_ref)
    for c in range(3):
        out_ref[c : c + 1, :] = x[c]
        out_ref[3 + c : 4 + c, :] = force[c]
    out_ref[6:ROWS, :] = jnp.zeros((ROWS - 6, x[0].shape[1]), jnp.float32)


def last_kernel(others, scale, *refs):
    own_ref, column_ref, start_ref, position_ref, velocity_ref, sum_ref = refs[others:]
    pair_sums(refs[:others], column_ref, start_ref, sum_ref)
    velocity = velocity_rows(sum_ref, scale)
    position_ref[...] = own_ref[0:3, :]
    for c in range(3):
        velocity_ref[c : c + 1, :] = velocity[c]


def exchange(block, axis):
    size = lax.axis_size(axis)
    return [
        lax.ppermute(
            block, axis, [(i, (i + shift) % size if size & (size - 1) else i ^ shift) for i in range(size)]
        )
        for shift in range(1, size)
    ]


def near_sums(near, state):
    nodes = state.shape[1]
    shape = jax.ShapeDtypeStruct((3, nodes, LANES), jnp.float32)
    pairs = near.shape[0] * nodes * nodes
    return pl.pallas_call(
        near_kernel,
        out_shape=(shape, shape),
        in_specs=[VMEM] * 2,
        out_specs=(VMEM,) * 2,
        compiler_params=GRANT,
        cost_estimate=pl.CostEstimate(flops=31 * pairs, bytes_accessed=8 * 3 * nodes * LANES, transcendentals=pairs),
    )(near, state)


def body(positions, forces, neighbours, patch_owner, rest_length, moduli, rest_bend):
    devices = lax.axis_size("tgt") * lax.axis_size("src")
    nodes = positions.shape[1]
    scale = 1.0 / math.sqrt(devices * nodes)
    slots = lax.all_to_all(
        pack_slots(rest_length, moduli, rest_bend, devices), AXES, split_axis=0, concat_axis=0, tiled=True
    )
    state = jnp.concatenate([positions, forces, jnp.zeros((ROWS - 6, nodes), jnp.float32)], axis=0)
    params = pick_slots(slots, patch_owner.reshape(1, nodes), rest_length.shape[1] // devices)
    sums = [pltpu.VMEM((3, nodes, LANES), jnp.float32)]
    for step in range(STEPS + 1):
        near = jnp.stack([state] + exchange(state, "src"))
        far = exchange(near, "tgt")
        column, start = near_sums(near, state)
        if step < STEPS:
            state = pl.pallas_call(
                functools.partial(step_kernel, len(far), scale),
                out_shape=jax.ShapeDtypeStruct((ROWS, nodes), jnp.float32),
                in_specs=[VMEM] * (len(far) + 5),
                out_specs=VMEM,
                scratch_shapes=sums,
                compiler_params=GRANT,
            )(*far, state, column, start, neighbours, params)
    return pl.pallas_call(
        functools.partial(last_kernel, len(far), scale),
        out_shape=(jax.ShapeDtypeStruct((3, nodes), jnp.float32),) * 2,
        in_specs=[VMEM] * (len(far) + 3),
        out_specs=(VMEM,) * 2,
        scratch_shapes=sums,
        compiler_params=GRANT,
    )(*far, state, column, start)


def solution(mesh):
    placed = (
        P(None, AXES),
        P(None, AXES),
        P(None, AXES),
        P(AXES, None),
        P(None, AXES),
        P(None, AXES),
        P(None, AXES),
    )
    return jax.shard_map(
        body,
        mesh=mesh,
        in_specs=placed,
        out_specs=(P(None, AXES), P(None, AXES)),
        check_vma=False,
    )
```

```python
import functools
import math

import jax
import jax.numpy as jnp
from jax import lax
from jax.experimental import pallas as pl
from jax.experimental.pallas import tpu as pltpu
from jax.sharding import PartitionSpec as P

STEPS = 3
LANES = 128
ROWS = 8
TARGET_ROWS = 32
PARAMS = 16

blob_square = 0.0025
time_step = 0.5

AXES = ("tgt", "src")
VMEM = pl.BlockSpec(memory_space=pltpu.VMEM)
GRANT = pltpu.CompilerParams(vmem_limit_bytes=32 * 1024 * 1024)


def pack_kernel(length_ref, moduli_ref, bend_ref, out_ref):
    devices = out_ref.shape[0]
    capacity = length_ref.shape[1] // devices
    out_ref[...] = jnp.zeros(out_ref.shape, jnp.float32)
    for device in range(devices):
        cut = slice(device * capacity, (device + 1) * capacity)
        out_ref[device, 0:6, 0:capacity] = length_ref[:, cut]
        out_ref[device, 6:8, 0:capacity] = moduli_ref[:, cut]
        out_ref[device, 0:3, capacity : 2 * capacity] = bend_ref[:, cut]


def pack_slots(rest_length, moduli, rest_bend, devices):
    return pl.pallas_call(
        pack_kernel,
        out_shape=jax.ShapeDtypeStruct((devices, ROWS, LANES), jnp.float32),
        in_specs=[VMEM] * 3,
        out_specs=VMEM,
        compiler_params=GRANT,
    )(rest_length, moduli, rest_bend)


def pick_kernel(capacity, slots_ref, owner_ref, out_ref):
    devices = slots_ref.shape[0]
    nodes = owner_ref.shape[1]
    owner = owner_ref[...]
    across = jnp.broadcast_to(owner, (nodes, nodes))
    down = across.T
    earlier = lax.broadcasted_iota(jnp.int32, (nodes, nodes), 0) < lax.broadcasted_iota(
        jnp.int32, (nodes, nodes), 1
    )
    rank = jnp.sum(jnp.where((across == down) & earlier, 1, 0), axis=0, keepdims=True)
    for at in range(0, nodes, LANES):
        place = jnp.broadcast_to(rank[:, at : at + LANES], (ROWS, LANES))
        named = jnp.broadcast_to(owner[:, at : at + LANES], (ROWS, LANES))
        for part in range(PARAMS // ROWS):

            def choose(device, chosen):
                taken = jnp.take_along_axis(
                    slots_ref[device], place + part * capacity, axis=1, mode="promise_in_bounds"
                )
                return jnp.where(named == device, taken, chosen)

            out_ref[part * ROWS : (part + 1) * ROWS, at : at + LANES] = lax.fori_loop(
                0, devices, choose, jnp.zeros((ROWS, LANES), jnp.float32), unroll=4
            )


def pick_slots(slots, owner, capacity):
    return pl.pallas_call(
        functools.partial(pick_kernel, capacity),
        out_shape=jax.ShapeDtypeStruct((PARAMS, owner.shape[1]), jnp.float32),
        in_specs=[VMEM] * 2,
        out_specs=VMEM,
        compiler_params=GRANT,
    )(slots, owner)


def spread_columns(own_ref, column_ref):
    for c in range(3):
        for at in range(0, own_ref.shape[1], LANES):
            row = own_ref[c : c + 1, at : at + LANES]
            column_ref[c, at : at + LANES, :] = jnp.broadcast_to(row, (LANES, LANES)).T


def pair_sums(source_refs, column_ref, start_ref, sum_ref):
    nodes = column_ref.shape[1]

    def per_target(block, _):
        rows = pl.ds(pl.multiple_of(block * TARGET_ROWS, TARGET_ROWS), TARGET_ROWS)
        target = [column_ref[c, rows, :] for c in range(3)]
        if start_ref is None:
            totals = (jnp.zeros((TARGET_ROWS, LANES), jnp.float32),) * 3
        else:
            totals = tuple(start_ref[c, rows, :] for c in range(3))
        for source_ref in source_refs:

            def per_source(device, totals):
                for at in range(0, nodes, LANES):
                    x = [source_ref[device, c : c + 1, at : at + LANES] for c in range(3)]
                    f = [source_ref[device, 3 + c : 4 + c, at : at + LANES] for c in range(3)]
                    d = [target[c] - x[c] for c in range(3)]
                    shifted = d[0] * d[0] + (d[1] * d[1] + (d[2] * d[2] + blob_square))
                    r = lax.rsqrt(shifted)
                    cube = r * (r * r)
                    direct = r + blob_square * cube
                    along = (d[0] * f[0] + d[1] * f[1] + d[2] * f[2]) * cube
                    totals = tuple(totals[c] + (direct * f[c] + along * d[c]) for c in range(3))
                return totals

            totals = lax.fori_loop(0, source_ref.shape[0], per_source, totals, unroll=2)
        for c in range(3):
            sum_ref[c, rows, :] = totals[c]
        return 0

    lax.fori_loop(0, nodes // TARGET_ROWS, per_target, 0)


def velocity_rows(sum_ref, scale):
    nodes = sum_ref.shape[1]
    velocity = []
    for c in range(3):
        parts = [
            jnp.sum(sum_ref[c, at : at + LANES, :].T, axis=0, keepdims=True)
            for at in range(0, nodes, LANES)
        ]
        velocity.append(jnp.concatenate(parts, axis=1) * scale)
    return velocity


def membrane(x, neighbours_ref, params_ref):
    nodes = x[0].shape[1]
    force = [[], [], []]
    for at in range(0, nodes, LANES):
        here = slice(at, at + LANES)
        points = [neighbours_ref[0:6, here], neighbours_ref[6:12, here]]
        edges = []
        for index in points:
            local = index & (LANES - 1)
            group = index // LANES
            component = []
            for c in range(3):
                found = jnp.zeros(index.shape, jnp.float32)
                for part in range(nodes // LANES):
                    source = jnp.broadcast_to(x[c][:, part * LANES : (part + 1) * LANES], index.shape)
                    taken = jnp.take_along_axis(source, local, axis=1, mode="promise_in_bounds")
                    found = jnp.where(group == part, taken, found)
                component.append(found - x[c][:, here])
            edges.append(component)
        near, far = edges
        length = params_ref[0:6, here]
        stretch = (near[0] * near[0] + near[1] * near[1] + near[2] * near[2]) / (length * length)
        tension = (stretch - 1.0) / (stretch + 1.0) / length
        for c in range(3):
            surface = jnp.sum(tension * near[c], axis=0, keepdims=True)
            bending = jnp.sum((2.0 / 9.0) * near[c] - (1.0 / 18.0) * far[c], axis=0, keepdims=True)
            bending = bending - params_ref[8 + c : 9 + c, here]
            force[c].append(params_ref[6:7, here] * surface + params_ref[7:8, here] * bending)
    return [jnp.concatenate(parts, axis=1) for parts in force]


def near_kernel(source_ref, own_ref, column_ref, sum_ref):
    spread_columns(own_ref, column_ref)
    pair_sums([source_ref], column_ref, None, sum_ref)


def step_kernel(others, scale, *refs):
    own_ref, column_ref, start_ref, neighbours_ref, params_ref, out_ref, sum_ref = refs[others:]
    pair_sums(refs[:others], column_ref, start_ref, sum_ref)
    velocity = velocity_rows(sum_ref, scale)
    x = [own_ref[c : c + 1, :] + time_step * velocity[c] for c in range(3)]
    force = membrane(x, neighbours_ref, params_ref)
    for c in range(3):
        out_ref[c : c + 1, :] = x[c]
        out_ref[3 + c : 4 + c, :] = force[c]
    out_ref[6:ROWS, :] = jnp.zeros((ROWS - 6, x[0].shape[1]), jnp.float32)


def last_kernel(others, scale, *refs):
    own_ref, column_ref, start_ref, position_ref, velocity_ref, sum_ref = refs[others:]
    pair_sums(refs[:others], column_ref, start_ref, sum_ref)
    velocity = velocity_rows(sum_ref, scale)
    position_ref[...] = own_ref[0:3, :]
    for c in range(3):
        velocity_ref[c : c + 1, :] = velocity[c]


def spread(state, devices):
    parities = [list(range(parity, devices, 2)) for parity in range(2)]
    copies = jnp.broadcast_to(state[None], (devices // 2,) + state.shape)
    near = lax.all_to_all(copies, AXES, split_axis=0, concat_axis=0, axis_index_groups=parities, tiled=True)
    far = lax.ppermute(near, AXES, [(i, i ^ 1) for i in range(devices)])
    return near, far


def near_sums(near, state):
    nodes = state.shape[1]
    shape = jax.ShapeDtypeStruct((3, nodes, LANES), jnp.float32)
    pairs = near.shape[0] * nodes * nodes
    return pl.pallas_call(
        near_kernel,
        out_shape=(shape, shape),
        in_specs=[VMEM] * 2,
        out_specs=(VMEM,) * 2,
        compiler_params=GRANT,
        cost_estimate=pl.CostEstimate(flops=31 * pairs, bytes_accessed=8 * 3 * nodes * LANES, transcendentals=pairs),
    )(near, state)


def body(positions, forces, neighbours, patch_owner, rest_length, moduli, rest_bend):
    devices = lax.axis_size("tgt") * lax.axis_size("src")
    nodes = positions.shape[1]
    scale = 1.0 / math.sqrt(devices * nodes)
    state = jnp.concatenate([positions, forces, jnp.zeros((ROWS - 6, nodes), jnp.float32)], axis=0)
    sums = [pltpu.VMEM((3, nodes, LANES), jnp.float32)]
    for step in range(STEPS + 1):
        near, far = spread(state, devices)
        if step == 0:
            packed = pack_slots(rest_length, moduli, rest_bend, devices)
            near, far, packed = lax.optimization_barrier((near, far, packed))
            slots = lax.all_to_all(packed, AXES, split_axis=0, concat_axis=0, tiled=True)
            params = pick_slots(slots, patch_owner.reshape(1, nodes), rest_length.shape[1] // devices)
        column, start = near_sums(near, state)
        if step < STEPS:
            state = pl.pallas_call(
                functools.partial(step_kernel, 1, scale),
                out_shape=jax.ShapeDtypeStruct((ROWS, nodes), jnp.float32),
                in_specs=[VMEM] * (6),
                out_specs=VMEM,
                scratch_shapes=sums,
                compiler_params=GRANT,
            )(far, state, column, start, neighbours, params)
    return pl.pallas_call(
        functools.partial(last_kernel, 1, scale),
        out_shape=(jax.ShapeDtypeStruct((3, nodes), jnp.float32),) * 2,
        in_specs=[VMEM] * (4),
        out_specs=(VMEM,) * 2,
        scratch_shapes=sums,
        compiler_params=GRANT,
    )(far, state, column, start)


def solution(mesh):
    placed = (
        P(None, AXES),
        P(None, AXES),
        P(None, AXES),
        P(AXES, None),
        P(None, AXES),
        P(None, AXES),
        P(None, AXES),
    )
    return jax.shard_map(
        body,
        mesh=mesh,
        in_specs=placed,
        out_specs=(P(None, AXES), P(None, AXES)),
        check_vma=False,
    )
```

```python
import functools
import math

import jax
import jax.numpy as jnp
from jax import lax
from jax.experimental import pallas as pl
from jax.experimental.pallas import tpu as pltpu
from jax.sharding import PartitionSpec as P

STEPS = 3
LANES = 128
ROWS = 8
TARGET_ROWS = 32
PARAMS = 16

blob_square = 0.0025
time_step = 0.5

AXES = ("tgt", "src")
VMEM = pl.BlockSpec(memory_space=pltpu.VMEM)
GRANT = pltpu.CompilerParams(vmem_limit_bytes=32 * 1024 * 1024)


def pack_kernel(length_ref, moduli_ref, bend_ref, out_ref):
    devices = out_ref.shape[0]
    capacity = length_ref.shape[1] // devices
    out_ref[...] = jnp.zeros(out_ref.shape, jnp.float32)
    for device in range(devices):
        cut = slice(device * capacity, (device + 1) * capacity)
        out_ref[device, 0:6, 0:capacity] = length_ref[:, cut]
        out_ref[device, 6:8, 0:capacity] = moduli_ref[:, cut]
        out_ref[device, 0:3, capacity : 2 * capacity] = bend_ref[:, cut]


def pack_slots(rest_length, moduli, rest_bend, devices):
    return pl.pallas_call(
        pack_kernel,
        out_shape=jax.ShapeDtypeStruct((devices, ROWS, LANES), jnp.float32),
        in_specs=[VMEM] * 3,
        out_specs=VMEM,
        compiler_params=GRANT,
    )(rest_length, moduli, rest_bend)


def pick_kernel(capacity, slots_ref, owner_ref, out_ref):
    devices = slots_ref.shape[0]
    nodes = owner_ref.shape[1]
    owner = owner_ref[...]
    across = jnp.broadcast_to(owner, (nodes, nodes))
    down = across.T
    earlier = lax.broadcasted_iota(jnp.int32, (nodes, nodes), 0) < lax.broadcasted_iota(
        jnp.int32, (nodes, nodes), 1
    )
    rank = jnp.sum(jnp.where((across == down) & earlier, 1, 0), axis=0, keepdims=True)
    for at in range(0, nodes, LANES):
        place = jnp.broadcast_to(rank[:, at : at + LANES], (ROWS, LANES))
        named = jnp.broadcast_to(owner[:, at : at + LANES], (ROWS, LANES))
        for part in range(PARAMS // ROWS):

            def choose(device, chosen):
                taken = jnp.take_along_axis(
                    slots_ref[device], place + part * capacity, axis=1, mode="promise_in_bounds"
                )
                return jnp.where(named == device, taken, chosen)

            out_ref[part * ROWS : (part + 1) * ROWS, at : at + LANES] = lax.fori_loop(
                0, devices, choose, jnp.zeros((ROWS, LANES), jnp.float32), unroll=4
            )


def pick_slots(slots, owner, capacity):
    return pl.pallas_call(
        functools.partial(pick_kernel, capacity),
        out_shape=jax.ShapeDtypeStruct((PARAMS, owner.shape[1]), jnp.float32),
        in_specs=[VMEM] * 2,
        out_specs=VMEM,
        compiler_params=GRANT,
    )(slots, owner)


def spread_columns(own_ref, column_ref):
    for c in range(3):
        for at in range(0, own_ref.shape[1], LANES):
            row = own_ref[c : c + 1, at : at + LANES]
            column_ref[c, at : at + LANES, :] = jnp.broadcast_to(row, (LANES, LANES)).T


def pair_sums(source_refs, column_ref, start_ref, sum_ref):
    nodes = column_ref.shape[1]

    def per_target(block, _):
        rows = pl.ds(pl.multiple_of(block * TARGET_ROWS, TARGET_ROWS), TARGET_ROWS)
        target = [column_ref[c, rows, :] for c in range(3)]
        if start_ref is None:
            totals = (jnp.zeros((TARGET_ROWS, LANES), jnp.float32),) * 3
        else:
            totals = tuple(start_ref[c, rows, :] for c in range(3))
        for source_ref in source_refs:

            def per_source(device, totals):
                for at in range(0, nodes, LANES):
                    x = [source_ref[device, c : c + 1, at : at + LANES] for c in range(3)]
                    f = [source_ref[device, 3 + c : 4 + c, at : at + LANES] for c in range(3)]
                    d = [target[c] - x[c] for c in range(3)]
                    shifted = d[0] * d[0] + (d[1] * d[1] + (d[2] * d[2] + blob_square))
                    r = lax.rsqrt(shifted)
                    cube = r * (r * r)
                    direct = r + blob_square * cube
                    along = (d[0] * f[0] + d[1] * f[1] + d[2] * f[2]) * cube
                    totals = tuple(totals[c] + (direct * f[c] + along * d[c]) for c in range(3))
                return totals

            totals = lax.fori_loop(0, source_ref.shape[0], per_source, totals, unroll=min(2, source_ref.shape[0]))
        for c in range(3):
            sum_ref[c, rows, :] = totals[c]
        return 0

    lax.fori_loop(0, nodes // TARGET_ROWS, per_target, 0)


def velocity_rows(sum_ref, scale):
    nodes = sum_ref.shape[1]
    velocity = []
    for c in range(3):
        parts = [
            jnp.sum(sum_ref[c, at : at + LANES, :].T, axis=0, keepdims=True)
            for at in range(0, nodes, LANES)
        ]
        velocity.append(jnp.concatenate(parts, axis=1) * scale)
    return velocity


def membrane(x, neighbours_ref, params_ref):
    nodes = x[0].shape[1]
    force = [[], [], []]
    for at in range(0, nodes, LANES):
        here = slice(at, at + LANES)
        points = [neighbours_ref[0:6, here], neighbours_ref[6:12, here]]
        edges = []
        for index in points:
            local = index & (LANES - 1)
            group = index // LANES
            component = []
            for c in range(3):
                found = jnp.zeros(index.shape, jnp.float32)
                for part in range(nodes // LANES):
                    source = jnp.broadcast_to(x[c][:, part * LANES : (part + 1) * LANES], index.shape)
                    taken = jnp.take_along_axis(source, local, axis=1, mode="promise_in_bounds")
                    found = jnp.where(group == part, taken, found)
                component.append(found - x[c][:, here])
            edges.append(component)
        near, far = edges
        length = params_ref[0:6, here]
        stretch = (near[0] * near[0] + near[1] * near[1] + near[2] * near[2]) / (length * length)
        tension = (stretch - 1.0) / (stretch + 1.0) / length
        for c in range(3):
            surface = jnp.sum(tension * near[c], axis=0, keepdims=True)
            bending = jnp.sum((2.0 / 9.0) * near[c] - (1.0 / 18.0) * far[c], axis=0, keepdims=True)
            bending = bending - params_ref[8 + c : 9 + c, here]
            force[c].append(params_ref[6:7, here] * surface + params_ref[7:8, here] * bending)
    return [jnp.concatenate(parts, axis=1) for parts in force]


def first_kernel(source_ref, column_ref, sum_ref):
    spread_columns(source_ref.at[0], column_ref)
    pair_sums([source_ref], column_ref, None, sum_ref)


def more_kernel(source_ref, column_ref, start_ref, sum_ref):
    pair_sums([source_ref], column_ref, start_ref, sum_ref)


def step_kernel(scale, source_ref, own_ref, column_ref, start_ref, neighbours_ref, params_ref, out_ref, sum_ref):
    pair_sums([source_ref], column_ref, start_ref, sum_ref)
    velocity = velocity_rows(sum_ref, scale)
    x = [own_ref[0, c : c + 1, :] + time_step * velocity[c] for c in range(3)]
    force = membrane(x, neighbours_ref, params_ref)
    for c in range(3):
        out_ref[0, c : c + 1, :] = x[c]
        out_ref[0, 3 + c : 4 + c, :] = force[c]
    out_ref[0, 6:ROWS, :] = jnp.zeros((ROWS - 6, x[0].shape[1]), jnp.float32)


def last_kernel(scale, source_ref, own_ref, column_ref, start_ref, position_ref, velocity_ref, sum_ref):
    pair_sums([source_ref], column_ref, start_ref, sum_ref)
    velocity = velocity_rows(sum_ref, scale)
    position_ref[...] = own_ref[0, 0:3, :]
    for c in range(3):
        velocity_ref[c : c + 1, :] = velocity[c]


def call(kernel, out_shape, operands, sources, scratch=()):
    nodes = sources.shape[2]
    pairs = sources.shape[0] * nodes * nodes
    return pl.pallas_call(
        kernel,
        out_shape=out_shape,
        in_specs=[VMEM] * len(operands),
        out_specs=jax.tree.map(lambda _: VMEM, out_shape),
        scratch_shapes=scratch,
        compiler_params=GRANT,
        cost_estimate=pl.CostEstimate(flops=31 * pairs, bytes_accessed=8 * 3 * nodes * LANES, transcendentals=pairs),
    )(*operands)


def exchange_order(devices):
    return [1 << bit for bit in range(1, devices.bit_length() - 1)] + [1]


def body(positions, forces, neighbours, patch_owner, rest_length, moduli, rest_bend):
    devices = lax.axis_size("tgt") * lax.axis_size("src")
    nodes = positions.shape[1]
    scale = 1.0 / math.sqrt(devices * nodes)
    sums = jax.ShapeDtypeStruct((3, nodes, LANES), jnp.float32)
    row = jax.ShapeDtypeStruct((3, nodes), jnp.float32)
    slots = lax.all_to_all(
        pack_slots(rest_length, moduli, rest_bend, devices), AXES, split_axis=0, concat_axis=0, tiled=True
    )
    params = pick_slots(slots, patch_owner.reshape(1, nodes), rest_length.shape[1] // devices)
    state = jnp.concatenate([positions, forces, jnp.zeros((ROWS - 6, nodes), jnp.float32)], axis=0)[None]
    scratch = [pltpu.VMEM(sums.shape, jnp.float32)]
    for step in range(STEPS + 1):
        held = newest = state
        column = total = None
        for distance in exchange_order(devices):
            arriving = lax.ppermute(held, AXES, [(i, i ^ distance) for i in range(devices)])
            if total is None:
                column, total = call(first_kernel, (sums, sums), (newest,), newest)
            else:
                total = call(more_kernel, sums, (newest, column, total), newest)
            arriving, total = lax.optimization_barrier((arriving, total))
            held = jnp.concatenate([held, arriving], axis=0)
            newest = arriving
        if step < STEPS:
            state = call(
                functools.partial(step_kernel, scale),
                jax.ShapeDtypeStruct((1, ROWS, nodes), jnp.float32),
                (newest, state, column, total, neighbours, params),
                newest,
                scratch,
            )
    return call(functools.partial(last_kernel, scale), (row, row), (newest, state, column, total), newest, scratch)


def solution(mesh):
    placed = (
        P(None, AXES),
        P(None, AXES),
        P(None, AXES),
        P(AXES, None),
        P(None, AXES),
        P(None, AXES),
        P(None, AXES),
    )
    return jax.shard_map(
        body,
        mesh=mesh,
        in_specs=placed,
        out_specs=(P(None, AXES), P(None, AXES)),
        check_vma=False,
    )
```

```python
import functools
import math

import jax
import jax.numpy as jnp
from jax import lax
from jax.experimental import pallas as pl
from jax.experimental.pallas import tpu as pltpu
from jax.sharding import PartitionSpec as P

STEPS = 3
LANES = 128
ROWS = 8
TARGET_ROWS = 32
PARAMS = 16

blob_square = 0.0025
time_step = 0.5

AXES = ("tgt", "src")
VMEM = pl.BlockSpec(memory_space=pltpu.VMEM)
GRANT = pltpu.CompilerParams(vmem_limit_bytes=32 * 1024 * 1024)


def pack_kernel(*refs):
    inputs, (out_ref, state_ref), copies, semaphores = refs[:5], refs[5:7], refs[7:12], refs[12]
    loads = [pltpu.make_async_copy(inputs[i], copies[i], semaphores.at[i]) for i in range(5)]
    for load in loads:
        load.start()
    for load in loads:
        load.wait()
    position_ref, force_ref, length_ref, moduli_ref, bend_ref = copies
    chips = out_ref.shape[0]
    nodes = position_ref.shape[1]
    capacity = length_ref.shape[1] // (2 * chips)
    state = jnp.concatenate(
        [position_ref[...], force_ref[...], jnp.zeros((ROWS - 6, nodes), jnp.float32)], axis=0
    )
    state_ref[...] = state
    for chip in range(chips):
        out_ref[chip, 0:ROWS, :] = state
        for core in range(2):
            start = (2 * chip + core) * capacity
            cut = slice(start, start + capacity)
            lane = core * LANES
            out_ref[chip, 8:14, lane : lane + capacity] = length_ref[:, cut]
            out_ref[chip, 14:16, lane : lane + capacity] = moduli_ref[:, cut]
            out_ref[chip, 8:11, lane + capacity : lane + 2 * capacity] = bend_ref[:, cut]


def pack(positions, forces, rest_length, moduli, rest_bend, devices):
    operands = (positions, forces, rest_length, moduli, rest_bend)
    nodes = positions.shape[1]
    return pl.pallas_call(
        pack_kernel,
        out_shape=(
            jax.ShapeDtypeStruct((devices // 2, 2 * ROWS, 2 * LANES), jnp.float32),
            jax.ShapeDtypeStruct((ROWS, nodes), jnp.float32),
        ),
        in_specs=[pl.BlockSpec(memory_space=pl.ANY)] * 5,
        out_specs=(VMEM,) * 2,
        scratch_shapes=[pltpu.VMEM(x.shape, x.dtype) for x in operands] + [pltpu.SemaphoreType.DMA((5,))],
        compiler_params=pltpu.CompilerParams(vmem_limit_bytes=60 * 1024 * 1024),
    )(*operands)


def pick_slots(capacity, near_ref, far_ref, owner_ref, params_ref):
    chips = near_ref.shape[0]
    nodes = owner_ref.shape[1]
    owner = owner_ref[...]
    across = jnp.broadcast_to(owner, (nodes, nodes))
    earlier = lax.broadcasted_iota(jnp.int32, (nodes, nodes), 0) < lax.broadcasted_iota(
        jnp.int32, (nodes, nodes), 1
    )
    rank = jnp.sum(jnp.where((across == across.T) & earlier, 1, 0), axis=0, keepdims=True)
    parity = lax.axis_index("src") & 1
    lanes = pl.ds(pl.multiple_of(parity * LANES, LANES), LANES)
    spots = range(0, nodes, LANES)
    places = [jnp.broadcast_to(rank[:, at : at + LANES], (ROWS, LANES)) for at in spots]
    owners = [jnp.broadcast_to(owner[:, at : at + LANES], (ROWS, LANES)) for at in spots]

    def choose(chip, chosen):
        chosen = list(chosen)
        for ref, device in ((near_ref, 2 * chip + parity), (far_ref, 2 * chip + 1 - parity)):
            block = ref[chip, ROWS : 2 * ROWS, lanes]
            for i in range(len(spots)):
                for part in range(2):
                    taken = jnp.take_along_axis(
                        block, places[i] + part * capacity, axis=1, mode="promise_in_bounds"
                    )
                    at = 2 * i + part
                    chosen[at] = jnp.where(owners[i] == device, taken, chosen[at])
        return tuple(chosen)

    zero = jnp.zeros((ROWS, LANES), jnp.float32)
    chosen = lax.fori_loop(0, chips, choose, (zero,) * (2 * len(spots)), unroll=4)
    for i, at in enumerate(spots):
        for part in range(2):
            params_ref[part * ROWS : (part + 1) * ROWS, at : at + LANES] = chosen[2 * i + part]


def spread_columns(own_ref, column_ref):
    for c in range(3):
        for at in range(0, own_ref.shape[1], LANES):
            row = own_ref[c : c + 1, at : at + LANES]
            column_ref[c, at : at + LANES, :] = jnp.broadcast_to(row, (LANES, LANES)).T


def pair_sums(source_refs, column_ref, start_ref, sum_ref):
    nodes = column_ref.shape[1]

    def per_target(block, _):
        rows = pl.ds(pl.multiple_of(block * TARGET_ROWS, TARGET_ROWS), TARGET_ROWS)
        target = [column_ref[c, rows, :] for c in range(3)]
        if start_ref is None:
            totals = (jnp.zeros((TARGET_ROWS, LANES), jnp.float32),) * 3
        else:
            totals = tuple(start_ref[c, rows, :] for c in range(3))
        for source_ref in source_refs:

            def per_source(device, totals):
                for at in range(0, nodes, LANES):
                    x = [source_ref[device, c : c + 1, at : at + LANES] for c in range(3)]
                    f = [source_ref[device, 3 + c : 4 + c, at : at + LANES] for c in range(3)]
                    d = [target[c] - x[c] for c in range(3)]
                    shifted = d[0] * d[0] + (d[1] * d[1] + (d[2] * d[2] + blob_square))
                    r = lax.rsqrt(shifted)
                    cube = r * (r * r)
                    direct = r + blob_square * cube
                    along = (d[0] * f[0] + d[1] * f[1] + d[2] * f[2]) * cube
                    totals = tuple(totals[c] + (direct * f[c] + along * d[c]) for c in range(3))
                return totals

            totals = lax.fori_loop(0, source_ref.shape[0], per_source, totals, unroll=2)
        for c in range(3):
            sum_ref[c, rows, :] = totals[c]
        return 0

    lax.fori_loop(0, nodes // TARGET_ROWS, per_target, 0)


def velocity_rows(sum_ref, scale):
    nodes = sum_ref.shape[1]
    velocity = []
    for c in range(3):
        parts = [
            jnp.sum(sum_ref[c, at : at + LANES, :].T, axis=0, keepdims=True)
            for at in range(0, nodes, LANES)
        ]
        velocity.append(jnp.concatenate(parts, axis=1) * scale)
    return velocity


def membrane(x, neighbours_ref, params_ref):
    nodes = x[0].shape[1]
    force = [[], [], []]
    for at in range(0, nodes, LANES):
        here = slice(at, at + LANES)
        points = [neighbours_ref[0:6, here], neighbours_ref[6:12, here]]
        edges = []
        for index in points:
            local = index & (LANES - 1)
            group = index // LANES
            component = []
            for c in range(3):
                found = jnp.zeros(index.shape, jnp.float32)
                for part in range(nodes // LANES):
                    source = jnp.broadcast_to(x[c][:, part * LANES : (part + 1) * LANES], index.shape)
                    taken = jnp.take_along_axis(source, local, axis=1, mode="promise_in_bounds")
                    found = jnp.where(group == part, taken, found)
                component.append(found - x[c][:, here])
            edges.append(component)
        near, far = edges
        length = params_ref[0:6, here]
        stretch = (near[0] * near[0] + near[1] * near[1] + near[2] * near[2]) / (length * length)
        tension = (stretch - 1.0) / (stretch + 1.0) / length
        for c in range(3):
            surface = jnp.sum(tension * near[c], axis=0, keepdims=True)
            bending = jnp.sum((2.0 / 9.0) * near[c] - (1.0 / 18.0) * far[c], axis=0, keepdims=True)
            bending = bending - params_ref[8 + c : 9 + c, here]
            force[c].append(params_ref[6:7, here] * surface + params_ref[7:8, here] * bending)
    return [jnp.concatenate(parts, axis=1) for parts in force]


def near_kernel(source_ref, own_ref, column_ref, sum_ref):
    spread_columns(own_ref, column_ref)
    pair_sums([source_ref], column_ref, None, sum_ref)


def advance(scale, own_ref, sum_ref, neighbours_ref, params_ref, out_ref):
    velocity = velocity_rows(sum_ref, scale)
    x = [own_ref[c : c + 1, :] + time_step * velocity[c] for c in range(3)]
    force = membrane(x, neighbours_ref, params_ref)
    for c in range(3):
        out_ref[c : c + 1, :] = x[c]
        out_ref[3 + c : 4 + c, :] = force[c]
    out_ref[6:ROWS, :] = jnp.zeros((ROWS - 6, x[0].shape[1]), jnp.float32)


def first_kernel(scale, capacity, *refs):
    far_ref, own_ref, column_ref, start_ref, neighbours_ref, near_ref, owner_ref, out_ref, params_ref, sum_ref = refs
    pick_slots(capacity, near_ref, far_ref, owner_ref, params_ref)
    pair_sums([far_ref], column_ref, start_ref, sum_ref)
    advance(scale, own_ref, sum_ref, neighbours_ref, params_ref, out_ref)


def step_kernel(scale, *refs):
    far_ref, own_ref, column_ref, start_ref, neighbours_ref, params_ref, out_ref, sum_ref = refs
    pair_sums([far_ref], column_ref, start_ref, sum_ref)
    advance(scale, own_ref, sum_ref, neighbours_ref, params_ref, out_ref)


def last_kernel(scale, *refs):
    far_ref, own_ref, column_ref, start_ref, position_ref, velocity_ref, sum_ref = refs
    pair_sums([far_ref], column_ref, start_ref, sum_ref)
    velocity = velocity_rows(sum_ref, scale)
    position_ref[...] = own_ref[0:3, :]
    for c in range(3):
        velocity_ref[c : c + 1, :] = velocity[c]


def spread(copies, devices):
    parities = [list(range(parity, devices, 2)) for parity in range(2)]
    near = lax.all_to_all(copies, AXES, split_axis=0, concat_axis=0, axis_index_groups=parities, tiled=True)
    far = lax.ppermute(near, AXES, [(i, i ^ 1) for i in range(devices)])
    return near, far


def near_sums(near, state):
    nodes = state.shape[1]
    shape = jax.ShapeDtypeStruct((3, nodes, LANES), jnp.float32)
    pairs = near.shape[0] * nodes * nodes
    return pl.pallas_call(
        near_kernel,
        out_shape=(shape, shape),
        in_specs=[VMEM] * 2,
        out_specs=(VMEM,) * 2,
        compiler_params=GRANT,
        cost_estimate=pl.CostEstimate(flops=31 * pairs, bytes_accessed=8 * 3 * nodes * LANES, transcendentals=pairs),
    )(near, state)


def call(kernel, out_shape, operands):
    nodes = operands[1].shape[1]
    return pl.pallas_call(
        kernel,
        out_shape=out_shape,
        in_specs=[VMEM] * len(operands),
        out_specs=jax.tree.map(lambda _: VMEM, out_shape),
        scratch_shapes=[pltpu.VMEM((3, nodes, LANES), jnp.float32)],
        compiler_params=GRANT,
    )(*operands)


def body(positions, forces, neighbours, patch_owner, rest_length, moduli, rest_bend):
    devices = lax.axis_size("tgt") * lax.axis_size("src")
    nodes = positions.shape[1]
    scale = 1.0 / math.sqrt(devices * nodes)
    capacity = rest_length.shape[1] // devices
    state_shape = jax.ShapeDtypeStruct((ROWS, nodes), jnp.float32)
    params_shape = jax.ShapeDtypeStruct((PARAMS, nodes), jnp.float32)
    row_shape = jax.ShapeDtypeStruct((3, nodes), jnp.float32)
    copies, state = pack(positions, forces, rest_length, moduli, rest_bend, devices)
    for step in range(STEPS + 1):
        near, far = spread(copies, devices)
        column, start = near_sums(near, state)
        operands = (far, state, column, start)
        if step == 0:
            state, params = call(
                functools.partial(first_kernel, scale, capacity),
                (state_shape, params_shape),
                operands + (neighbours, near, patch_owner.reshape(1, nodes)),
            )
        elif step < STEPS:
            state = call(functools.partial(step_kernel, scale), state_shape, operands + (neighbours, params))
        copies = jnp.broadcast_to(state[None], (devices // 2,) + state.shape)
    return call(functools.partial(last_kernel, scale), (row_shape, row_shape), operands)


def solution(mesh):
    placed = (
        P(None, AXES),
        P(None, AXES),
        P(None, AXES),
        P(AXES, None),
        P(None, AXES),
        P(None, AXES),
        P(None, AXES),
    )
    return jax.shard_map(
        body,
        mesh=mesh,
        in_specs=placed,
        out_specs=(P(None, AXES), P(None, AXES)),
        check_vma=False,
    )
```

```python
import functools
import math

import jax
import jax.numpy as jnp
from jax import lax
from jax.experimental import pallas as pl
from jax.experimental.pallas import tpu as pltpu
from jax.sharding import PartitionSpec as P

STEPS = 3
LANES = 128
ROWS = 8
TARGET_ROWS = 32
PARAMS = 12
FOLD = 4

blob_square = 0.0025
time_step = 0.5

AXES = ("tgt", "src")
VMEM = pl.BlockSpec(memory_space=pltpu.VMEM)
GRANT = pltpu.CompilerParams(vmem_limit_bytes=32 * 1024 * 1024)


def pack_kernel(*refs):
    inputs, out_ref, copies = refs[:5], refs[5], refs[6:11]
    slots_ref, semaphores = refs[11:]
    loads = [pltpu.make_async_copy(inputs[i], copies[i], semaphores.at[i]) for i in range(5)]
    for load in loads:
        load.start()
    for load in loads:
        load.wait()
    position_ref, force_ref, length_ref, moduli_ref, bend_ref = copies
    chips = out_ref.shape[0]
    nodes = position_ref.shape[1]
    capacity = length_ref.shape[1] // (2 * chips)
    state = [ref[c : c + 1, :] for ref in (position_ref, force_ref) for c in range(3)]
    slots_ref[0:6, :] = length_ref[...]
    slots_ref[6:8, :] = moduli_ref[...]
    slots_ref[8:11, :] = bend_ref[...]
    slots_ref[11:12, :] = bend_ref[0:1, :]
    for chip in range(chips):
        for c in range(6):
            out_ref[chip, :, c * nodes : (c + 1) * nodes] = state[c]
        for core in range(2):
            cut = slice((2 * chip + core) * capacity, (2 * chip + core + 1) * capacity)
            for part in range(PARAMS // FOLD):
                rows = slots_ref[part * FOLD : (part + 1) * FOLD, cut]
                for t in range(FOLD):
                    lane = 6 * nodes + (core * FOLD + t) * LANES + part * capacity
                    out_ref[chip, :, lane : lane + capacity] = rows[t : t + 1, :]


def pack(positions, forces, rest_length, moduli, rest_bend, devices):
    operands = (positions, forces, rest_length, moduli, rest_bend)
    nodes = positions.shape[1]
    return pl.pallas_call(
        pack_kernel,
        out_shape=jax.ShapeDtypeStruct((devices // 2, 1, 6 * nodes + 2 * FOLD * LANES), jnp.float32),
        in_specs=[pl.BlockSpec(memory_space=pl.ANY)] * 5,
        out_specs=VMEM,
        scratch_shapes=[pltpu.VMEM(x.shape, x.dtype) for x in operands]
        + [pltpu.VMEM((PARAMS, rest_length.shape[1]), jnp.float32), pltpu.SemaphoreType.DMA((5,))],
        compiler_params=pltpu.CompilerParams(vmem_limit_bytes=60 * 1024 * 1024),
    )(*operands)


def pick_slots(capacity, near_ref, far_ref, owner_ref, params_ref):
    chips = near_ref.shape[0]
    nodes = owner_ref.shape[1]
    parts = PARAMS // FOLD
    owner = owner_ref[...]
    across = jnp.broadcast_to(owner, (nodes, nodes))
    earlier = lax.broadcasted_iota(jnp.int32, (nodes, nodes), 0) < lax.broadcasted_iota(
        jnp.int32, (nodes, nodes), 1
    )
    rank = jnp.sum(jnp.where((across == across.T) & earlier, 1, 0), axis=0, keepdims=True)
    parity = lax.axis_index("src") & 1
    spots = range(0, nodes, LANES)
    part = jnp.minimum(lax.broadcasted_iota(jnp.int32, (ROWS, LANES), 0), parts - 1)
    places = [rank[:, at : at + LANES] + part * capacity for at in spots]
    owners = [jnp.broadcast_to(owner[:, at : at + LANES], (ROWS, LANES)) for at in spots]

    def choose(chip, chosen):
        chosen = list(chosen)
        for ref, device in ((near_ref, 2 * chip + parity), (far_ref, 2 * chip + 1 - parity)):
            for t in range(FOLD):
                lane = pl.multiple_of(6 * nodes + (parity * FOLD + t) * LANES, LANES)
                block = jnp.broadcast_to(ref[chip, :, pl.ds(lane, LANES)], (ROWS, LANES))
                for i in range(len(spots)):
                    taken = jnp.take_along_axis(block, places[i], axis=1, mode="promise_in_bounds")
                    at = i * FOLD + t
                    chosen[at] = jnp.where(owners[i] == device, taken, chosen[at])
        return tuple(chosen)

    zero = jnp.zeros((ROWS, LANES), jnp.float32)
    chosen = lax.fori_loop(0, chips, choose, (zero,) * (FOLD * len(spots)), unroll=4)
    for i, at in enumerate(spots):
        for t in range(FOLD):
            for j in range(parts):
                params_ref[j * FOLD + t : j * FOLD + t + 1, at : at + LANES] = chosen[i * FOLD + t][j : j + 1, :]


def spread_columns(own_ref, column_ref):
    nodes = column_ref.shape[1]
    for c in range(3):
        for at in range(0, nodes, LANES):
            row = own_ref[0, :, c * nodes + at : c * nodes + at + LANES]
            column_ref[c, at : at + LANES, :] = jnp.broadcast_to(row, (LANES, LANES)).T


def pair_sums(source_refs, column_ref, start_ref, sum_ref):
    nodes = column_ref.shape[1]

    def per_target(block, _):
        rows = pl.ds(pl.multiple_of(block * TARGET_ROWS, TARGET_ROWS), TARGET_ROWS)
        target = [column_ref[c, rows, :] for c in range(3)]
        if start_ref is None:
            totals = (jnp.zeros((TARGET_ROWS, LANES), jnp.float32),) * 3
        else:
            totals = tuple(start_ref[c, rows, :] for c in range(3))
        for source_ref in source_refs:

            def per_source(device, totals):
                for at in range(0, nodes, LANES):
                    rows = [source_ref[device, :, c * nodes + at : c * nodes + at + LANES] for c in range(6)]
                    x, f = rows[:3], rows[3:]
                    d = [target[c] - x[c] for c in range(3)]
                    shifted = d[0] * d[0] + (d[1] * d[1] + (d[2] * d[2] + blob_square))
                    r = lax.rsqrt(shifted)
                    cube = r * (r * r)
                    direct = r + blob_square * cube
                    along = (d[0] * f[0] + d[1] * f[1] + d[2] * f[2]) * cube
                    totals = tuple(totals[c] + (direct * f[c] + along * d[c]) for c in range(3))
                return totals

            totals = lax.fori_loop(0, source_ref.shape[0], per_source, totals, unroll=2)
        for c in range(3):
            sum_ref[c, rows, :] = totals[c]
        return 0

    lax.fori_loop(0, nodes // TARGET_ROWS, per_target, 0)


def velocity_rows(sum_ref, scale):
    nodes = sum_ref.shape[1]
    velocity = []
    for c in range(3):
        parts = [
            jnp.sum(sum_ref[c, at : at + LANES, :].T, axis=0, keepdims=True)
            for at in range(0, nodes, LANES)
        ]
        velocity.append(jnp.concatenate(parts, axis=1) * scale)
    return velocity


def membrane(x, neighbours_ref, params_ref):
    nodes = x[0].shape[1]
    force = [[], [], []]
    for at in range(0, nodes, LANES):
        here = slice(at, at + LANES)
        points = [neighbours_ref[0:6, here], neighbours_ref[6:12, here]]
        edges = []
        for index in points:
            local = index & (LANES - 1)
            group = index // LANES
            component = []
            for c in range(3):
                found = jnp.zeros(index.shape, jnp.float32)
                for part in range(nodes // LANES):
                    source = jnp.broadcast_to(x[c][:, part * LANES : (part + 1) * LANES], index.shape)
                    taken = jnp.take_along_axis(source, local, axis=1, mode="promise_in_bounds")
                    found = jnp.where(group == part, taken, found)
                component.append(found - x[c][:, here])
            edges.append(component)
        near, far = edges
        length = params_ref[0:6, here]
        stretch = (near[0] * near[0] + near[1] * near[1] + near[2] * near[2]) / (length * length)
        tension = (stretch - 1.0) / (stretch + 1.0) / length
        for c in range(3):
            surface = jnp.sum(tension * near[c], axis=0, keepdims=True)
            bending = jnp.sum((2.0 / 9.0) * near[c] - (1.0 / 18.0) * far[c], axis=0, keepdims=True)
            bending = bending - params_ref[8 + c : 9 + c, here]
            force[c].append(params_ref[6:7, here] * surface + params_ref[7:8, here] * bending)
    return [jnp.concatenate(parts, axis=1) for parts in force]


def near_kernel(source_ref, own_ref, column_ref, sum_ref):
    spread_columns(own_ref, column_ref)
    pair_sums([source_ref], column_ref, None, sum_ref)


def advance(scale, own_ref, sum_ref, neighbours_ref, params_ref, out_ref):
    velocity = velocity_rows(sum_ref, scale)
    nodes = velocity[0].shape[1]
    x = [own_ref[0, :, c * nodes : (c + 1) * nodes] + time_step * velocity[c] for c in range(3)]
    force = membrane(x, neighbours_ref, params_ref)
    for chip in range(out_ref.shape[0]):
        for c in range(3):
            out_ref[chip, :, c * nodes : (c + 1) * nodes] = x[c]
            out_ref[chip, :, (3 + c) * nodes : (4 + c) * nodes] = force[c]


def first_kernel(scale, capacity, *refs):
    far_ref, own_ref, column_ref, start_ref, neighbours_ref, near_ref, owner_ref, out_ref, params_ref, sum_ref = refs
    pick_slots(capacity, near_ref, far_ref, owner_ref, params_ref)
    pair_sums([far_ref], column_ref, start_ref, sum_ref)
    advance(scale, own_ref, sum_ref, neighbours_ref, params_ref, out_ref)


def step_kernel(scale, *refs):
    far_ref, own_ref, column_ref, start_ref, neighbours_ref, params_ref, out_ref, sum_ref = refs
    pair_sums([far_ref], column_ref, start_ref, sum_ref)
    advance(scale, own_ref, sum_ref, neighbours_ref, params_ref, out_ref)


def last_kernel(scale, *refs):
    far_ref, own_ref, column_ref, start_ref, position_ref, velocity_ref, sum_ref = refs
    pair_sums([far_ref], column_ref, start_ref, sum_ref)
    velocity = velocity_rows(sum_ref, scale)
    nodes = velocity[0].shape[1]
    for c in range(3):
        position_ref[c : c + 1, :] = own_ref[0, :, c * nodes : (c + 1) * nodes]
        velocity_ref[c : c + 1, :] = velocity[c]


def spread(copies, devices):
    parities = [list(range(parity, devices, 2)) for parity in range(2)]
    near = lax.all_to_all(copies, AXES, split_axis=0, concat_axis=0, axis_index_groups=parities, tiled=True)
    far = lax.ppermute(near, AXES, [(i, i ^ 1) for i in range(devices)])
    return near, far


def near_sums(near, copies, nodes):
    shape = jax.ShapeDtypeStruct((3, nodes, LANES), jnp.float32)
    pairs = near.shape[0] * nodes * nodes
    return pl.pallas_call(
        near_kernel,
        out_shape=(shape, shape),
        in_specs=[VMEM] * 2,
        out_specs=(VMEM,) * 2,
        compiler_params=GRANT,
        cost_estimate=pl.CostEstimate(flops=31 * pairs, bytes_accessed=8 * 3 * nodes * LANES, transcendentals=pairs),
    )(near, copies)


def call(kernel, out_shape, operands, nodes):
    return pl.pallas_call(
        kernel,
        out_shape=out_shape,
        in_specs=[VMEM] * len(operands),
        out_specs=jax.tree.map(lambda _: VMEM, out_shape),
        scratch_shapes=[pltpu.VMEM((3, nodes, LANES), jnp.float32)],
        compiler_params=GRANT,
    )(*operands)


def body(positions, forces, neighbours, patch_owner, rest_length, moduli, rest_bend):
    devices = lax.axis_size("tgt") * lax.axis_size("src")
    nodes = positions.shape[1]
    scale = 1.0 / math.sqrt(devices * nodes)
    capacity = rest_length.shape[1] // devices
    copies_shape = jax.ShapeDtypeStruct((devices // 2, 1, 6 * nodes), jnp.float32)
    params_shape = jax.ShapeDtypeStruct((PARAMS, nodes), jnp.float32)
    row_shape = jax.ShapeDtypeStruct((3, nodes), jnp.float32)
    copies = pack(positions, forces, rest_length, moduli, rest_bend, devices)
    for step in range(STEPS + 1):
        near, far = spread(copies, devices)
        column, start = near_sums(near, copies, nodes)
        operands = (far, copies, column, start)
        if step == 0:
            copies, params = call(
                functools.partial(first_kernel, scale, capacity),
                (copies_shape, params_shape),
                operands + (neighbours, near, patch_owner.reshape(1, nodes)),
                nodes,
            )
        elif step < STEPS:
            operands = operands + (neighbours, params)
            copies = call(functools.partial(step_kernel, scale), copies_shape, operands, nodes)
    return call(functools.partial(last_kernel, scale), (row_shape, row_shape), operands, nodes)


def solution(mesh):
    placed = (
        P(None, AXES),
        P(None, AXES),
        P(None, AXES),
        P(AXES, None),
        P(None, AXES),
        P(None, AXES),
        P(None, AXES),
    )
    return jax.shard_map(
        body,
        mesh=mesh,
        in_specs=placed,
        out_specs=(P(None, AXES), P(None, AXES)),
        check_vma=False,
    )
```

```python
import functools
import math

import jax
import jax.numpy as jnp
from jax import lax
from jax.experimental import pallas as pl
from jax.experimental.pallas import tpu as pltpu
from jax.sharding import PartitionSpec as P

STEPS = 3
LANES = 128
ROWS = 8
TARGET_ROWS = 32
UNROLL = 8
PARAMS = 12
FOLD = 4

blob_square = 0.0025
inverse_blob = 20.0
time_step = 0.5

AXES = ("tgt", "src")
VMEM = pl.BlockSpec(memory_space=pltpu.VMEM)
GRANT = pltpu.CompilerParams(vmem_limit_bytes=32 * 1024 * 1024)


def pack_kernel(*refs):
    inputs, out_ref, copies = refs[:5], refs[5], refs[6:11]
    slots_ref, semaphores = refs[11:]
    loads = [pltpu.make_async_copy(inputs[i], copies[i], semaphores.at[i]) for i in range(5)]
    for load in loads:
        load.start()
    for load in loads:
        load.wait()
    position_ref, force_ref, length_ref, moduli_ref, bend_ref = copies
    chips = out_ref.shape[0]
    nodes = position_ref.shape[1]
    capacity = length_ref.shape[1] // (2 * chips)
    state = [inverse_blob * position_ref[c : c + 1, :] for c in range(3)]
    state += [force_ref[c : c + 1, :] for c in range(3)]
    slots_ref[0:6, :] = length_ref[...]
    slots_ref[6:8, :] = moduli_ref[...]
    slots_ref[8:11, :] = bend_ref[...]
    slots_ref[11:12, :] = bend_ref[0:1, :]
    for chip in range(chips):
        for c in range(6):
            out_ref[chip, :, c * nodes : (c + 1) * nodes] = state[c]
        for core in range(2):
            cut = slice((2 * chip + core) * capacity, (2 * chip + core + 1) * capacity)
            for part in range(PARAMS // FOLD):
                rows = slots_ref[part * FOLD : (part + 1) * FOLD, cut]
                for t in range(FOLD):
                    lane = 6 * nodes + (core * FOLD + t) * LANES + part * capacity
                    out_ref[chip, :, lane : lane + capacity] = rows[t : t + 1, :]


def pack(positions, forces, rest_length, moduli, rest_bend, devices):
    operands = (positions, forces, rest_length, moduli, rest_bend)
    nodes = positions.shape[1]
    return pl.pallas_call(
        pack_kernel,
        out_shape=jax.ShapeDtypeStruct((devices // 2, 1, 6 * nodes + 2 * FOLD * LANES), jnp.float32),
        in_specs=[pl.BlockSpec(memory_space=pl.ANY)] * 5,
        out_specs=VMEM,
        scratch_shapes=[pltpu.VMEM(x.shape, x.dtype) for x in operands]
        + [pltpu.VMEM((PARAMS, rest_length.shape[1]), jnp.float32), pltpu.SemaphoreType.DMA((5,))],
        compiler_params=pltpu.CompilerParams(vmem_limit_bytes=60 * 1024 * 1024),
    )(*operands)


def pick_slots(capacity, near_ref, far_ref, owner_ref, params_ref):
    chips = near_ref.shape[0]
    nodes = owner_ref.shape[1]
    parts = PARAMS // FOLD
    owner = owner_ref[...]
    across = jnp.broadcast_to(owner, (nodes, nodes))
    earlier = lax.broadcasted_iota(jnp.int32, (nodes, nodes), 0) < lax.broadcasted_iota(
        jnp.int32, (nodes, nodes), 1
    )
    rank = jnp.sum(jnp.where((across == across.T) & earlier, 1, 0), axis=0, keepdims=True)
    parity = lax.axis_index("src") & 1
    spots = range(0, nodes, LANES)
    part = jnp.minimum(lax.broadcasted_iota(jnp.int32, (ROWS, LANES), 0), parts - 1)
    places = [rank[:, at : at + LANES] + part * capacity for at in spots]
    owners = [jnp.broadcast_to(owner[:, at : at + LANES], (ROWS, LANES)) for at in spots]

    def choose(chip, chosen):
        chosen = list(chosen)
        for ref, device in ((near_ref, 2 * chip + parity), (far_ref, 2 * chip + 1 - parity)):
            for t in range(FOLD):
                lane = pl.multiple_of(6 * nodes + (parity * FOLD + t) * LANES, LANES)
                block = jnp.broadcast_to(ref[chip, :, pl.ds(lane, LANES)], (ROWS, LANES))
                for i in range(len(spots)):
                    taken = jnp.take_along_axis(block, places[i], axis=1, mode="promise_in_bounds")
                    at = i * FOLD + t
                    chosen[at] = jnp.where(owners[i] == device, taken, chosen[at])
        return tuple(chosen)

    zero = jnp.zeros((ROWS, LANES), jnp.float32)
    chosen = lax.fori_loop(0, chips, choose, (zero,) * (FOLD * len(spots)), unroll=4)
    for i, at in enumerate(spots):
        for t in range(FOLD):
            for j in range(parts):
                params_ref[j * FOLD + t : j * FOLD + t + 1, at : at + LANES] = chosen[i * FOLD + t][j : j + 1, :]


def spread_columns(own_ref, column_ref):
    nodes = column_ref.shape[1]
    for c in range(3):
        for at in range(0, nodes, LANES):
            row = own_ref[0, :, c * nodes + at : c * nodes + at + LANES]
            column_ref[c, at : at + LANES, :] = jnp.broadcast_to(row, (LANES, LANES)).T


def pair_sums(source_refs, column_ref, start_ref, sum_ref):
    nodes = column_ref.shape[1]

    def per_target(block, _):
        rows = pl.ds(pl.multiple_of(block * TARGET_ROWS, TARGET_ROWS), TARGET_ROWS)
        target = [column_ref[c, rows, :] for c in range(3)]
        if start_ref is None:
            totals = (jnp.zeros((TARGET_ROWS, LANES), jnp.float32),) * 3
        else:
            totals = tuple(start_ref[c, rows, :] for c in range(3))
        for source_ref in source_refs:

            def per_source(device, totals):
                for at in range(0, nodes, LANES):
                    rows = [source_ref[device, :, c * nodes + at : c * nodes + at + LANES] for c in range(6)]
                    x, f = rows[:3], rows[3:]
                    d = [target[c] - x[c] for c in range(3)]
                    shifted = d[0] * d[0] + (d[1] * d[1] + (d[2] * d[2] + 1.0))
                    r = lax.rsqrt(shifted)
                    cube = r * (r * r)
                    direct = r + cube
                    along = (d[0] * f[0] + d[1] * f[1] + d[2] * f[2]) * cube
                    totals = tuple(totals[c] + (direct * f[c] + along * d[c]) for c in range(3))
                return totals

            totals = lax.fori_loop(0, source_ref.shape[0], per_source, totals, unroll=2)
        for c in range(3):
            sum_ref[c, rows, :] = totals[c]
        return 0

    lax.fori_loop(0, nodes // TARGET_ROWS, per_target, 0)


def velocity_rows(sum_ref, scale):
    nodes = sum_ref.shape[1]
    velocity = []
    for c in range(3):
        parts = [
            jnp.sum(sum_ref[c, at : at + LANES, :].T, axis=0, keepdims=True)
            for at in range(0, nodes, LANES)
        ]
        velocity.append(jnp.concatenate(parts, axis=1) * (inverse_blob * scale))
    return velocity


def membrane(x, neighbours_ref, params_ref):
    nodes = x[0].shape[1]
    force = [[], [], []]
    for at in range(0, nodes, LANES):
        here = slice(at, at + LANES)
        points = [neighbours_ref[0:6, here], neighbours_ref[6:12, here]]
        edges = []
        for index in points:
            local = index & (LANES - 1)
            group = index // LANES
            component = []
            for c in range(3):
                found = jnp.zeros(index.shape, jnp.float32)
                for part in range(nodes // LANES):
                    source = jnp.broadcast_to(x[c][:, part * LANES : (part + 1) * LANES], index.shape)
                    taken = jnp.take_along_axis(source, local, axis=1, mode="promise_in_bounds")
                    found = jnp.where(group == part, taken, found)
                component.append(found - x[c][:, here])
            edges.append(component)
        near, far = edges
        length = params_ref[0:6, here]
        stretch = (near[0] * near[0] + near[1] * near[1] + near[2] * near[2]) / (length * length)
        tension = (stretch - 1.0) / (stretch + 1.0) / length
        for c in range(3):
            surface = jnp.sum(tension * near[c], axis=0, keepdims=True)
            bending = jnp.sum((2.0 / 9.0) * near[c] - (1.0 / 18.0) * far[c], axis=0, keepdims=True)
            bending = bending - params_ref[8 + c : 9 + c, here]
            force[c].append(params_ref[6:7, here] * surface + params_ref[7:8, here] * bending)
    return [jnp.concatenate(parts, axis=1) for parts in force]


def near_kernel(source_ref, own_ref, column_ref, sum_ref):
    spread_columns(own_ref, column_ref)
    pair_sums([source_ref], column_ref, None, sum_ref)


def advance(scale, position_ref, sum_ref, neighbours_ref, params_ref, out_ref, moved_ref):
    velocity = velocity_rows(sum_ref, scale)
    nodes = velocity[0].shape[1]
    x = [position_ref[c : c + 1, :] + time_step * velocity[c] for c in range(3)]
    for c in range(3):
        moved_ref[c : c + 1, :] = x[c]
    scaled = [inverse_blob * v for v in x]
    force = membrane(x, neighbours_ref, params_ref)
    for chip in range(out_ref.shape[0]):
        for c in range(3):
            out_ref[chip, :, c * nodes : (c + 1) * nodes] = scaled[c]
            out_ref[chip, :, (3 + c) * nodes : (4 + c) * nodes] = force[c]


def first_kernel(scale, capacity, *refs):
    far_ref, position_ref, column_ref, start_ref, neighbours_ref, near_ref, owner_ref = refs[:7]
    out_ref, moved_ref, params_ref, sum_ref = refs[7:]
    pick_slots(capacity, near_ref, far_ref, owner_ref, params_ref)
    pair_sums([far_ref], column_ref, start_ref, sum_ref)
    advance(scale, position_ref, sum_ref, neighbours_ref, params_ref, out_ref, moved_ref)


def step_kernel(scale, *refs):
    far_ref, position_ref, column_ref, start_ref, neighbours_ref, params_ref, out_ref, moved_ref, sum_ref = refs
    pair_sums([far_ref], column_ref, start_ref, sum_ref)
    advance(scale, position_ref, sum_ref, neighbours_ref, params_ref, out_ref, moved_ref)


def last_kernel(scale, far_ref, column_ref, start_ref, velocity_ref, sum_ref):
    pair_sums([far_ref], column_ref, start_ref, sum_ref)
    velocity = velocity_rows(sum_ref, scale)
    for c in range(3):
        velocity_ref[c : c + 1, :] = velocity[c]


def spread(copies, devices):
    parities = [list(range(parity, devices, 2)) for parity in range(2)]
    near = lax.all_to_all(copies, AXES, split_axis=0, concat_axis=0, axis_index_groups=parities, tiled=True)
    far = lax.ppermute(near, AXES, [(i, i ^ 1) for i in range(devices)])
    return near, far


def near_sums(near, copies, nodes):
    shape = jax.ShapeDtypeStruct((3, nodes, LANES), jnp.float32)
    pairs = near.shape[0] * nodes * nodes
    return pl.pallas_call(
        near_kernel,
        out_shape=(shape, shape),
        in_specs=[VMEM] * 2,
        out_specs=(VMEM,) * 2,
        compiler_params=GRANT,
        cost_estimate=pl.CostEstimate(flops=31 * pairs, bytes_accessed=8 * 3 * nodes * LANES, transcendentals=pairs),
    )(near, copies)


def call(kernel, out_shape, operands, nodes):
    return pl.pallas_call(
        kernel,
        out_shape=out_shape,
        in_specs=[VMEM] * len(operands),
        out_specs=jax.tree.map(lambda _: VMEM, out_shape),
        scratch_shapes=[pltpu.VMEM((3, nodes, LANES), jnp.float32)],
        compiler_params=GRANT,
    )(*operands)


def body(positions, forces, neighbours, patch_owner, rest_length, moduli, rest_bend):
    devices = lax.axis_size("tgt") * lax.axis_size("src")
    nodes = positions.shape[1]
    scale = 1.0 / math.sqrt(devices * nodes)
    capacity = rest_length.shape[1] // devices
    copies_shape = jax.ShapeDtypeStruct((devices // 2, 1, 6 * nodes), jnp.float32)
    params_shape = jax.ShapeDtypeStruct((PARAMS, nodes), jnp.float32)
    row_shape = jax.ShapeDtypeStruct((3, nodes), jnp.float32)
    position = positions
    copies = pack(positions, forces, rest_length, moduli, rest_bend, devices)
    for step in range(STEPS + 1):
        near, far = spread(copies, devices)
        column, start = near_sums(near, copies, nodes)
        operands = (far, position, column, start)
        if step == 0:
            copies, position, params = call(
                functools.partial(first_kernel, scale, capacity),
                (copies_shape, row_shape, params_shape),
                operands + (neighbours, near, patch_owner.reshape(1, nodes)),
                nodes,
            )
        elif step < STEPS:
            operands = operands + (neighbours, params)
            shapes = (copies_shape, row_shape)
            copies, position = call(functools.partial(step_kernel, scale), shapes, operands, nodes)
    velocity = call(functools.partial(last_kernel, scale), row_shape, (far, column, start), nodes)
    return position, velocity


def solution(mesh):
    placed = (
        P(None, AXES),
        P(None, AXES),
        P(None, AXES),
        P(AXES, None),
        P(None, AXES),
        P(None, AXES),
        P(None, AXES),
    )
    return jax.shard_map(
        body,
        mesh=mesh,
        in_specs=placed,
        out_specs=(P(None, AXES), P(None, AXES)),
        check_vma=False,
    )
```

```python
import functools
import math

import jax
import jax.numpy as jnp
from jax import lax
from jax.experimental import pallas as pl
from jax.experimental.pallas import tpu as pltpu
from jax.sharding import PartitionSpec as P

STEPS = 3
LANES = 128
ROWS = 8
TARGET_ROWS = 32
UNROLL = 16
PICK_UNROLL = 4
PARAMS = 12
FOLD = 4

blob_square = 0.0025
inverse_blob = 20.0
time_step = 0.5

AXES = ("tgt", "src")
VMEM = pl.BlockSpec(memory_space=pltpu.VMEM)
GRANT = pltpu.CompilerParams(vmem_limit_bytes=32 * 1024 * 1024)


def pack_kernel(*refs):
    inputs, out_ref, copies = refs[:5], refs[5], refs[6:11]
    slots_ref, semaphores = refs[11:]
    loads = [pltpu.make_async_copy(inputs[i], copies[i], semaphores.at[i]) for i in range(5)]
    for load in loads:
        load.start()
    for load in loads:
        load.wait()
    position_ref, force_ref, length_ref, moduli_ref, bend_ref = copies
    chips = out_ref.shape[0]
    nodes = position_ref.shape[1]
    capacity = length_ref.shape[1] // (2 * chips)
    state = [inverse_blob * position_ref[c : c + 1, :] for c in range(3)]
    state += [force_ref[c : c + 1, :] for c in range(3)]
    slots_ref[0:6, :] = length_ref[...]
    slots_ref[6:8, :] = moduli_ref[...]
    slots_ref[8:11, :] = bend_ref[...]
    slots_ref[11:12, :] = bend_ref[0:1, :]
    for chip in range(chips):
        for c in range(6):
            out_ref[chip, :, c * nodes : (c + 1) * nodes] = state[c]
        for core in range(2):
            cut = slice((2 * chip + core) * capacity, (2 * chip + core + 1) * capacity)
            for part in range(PARAMS // FOLD):
                rows = slots_ref[part * FOLD : (part + 1) * FOLD, cut]
                for t in range(FOLD):
                    lane = 6 * nodes + (core * FOLD + t) * LANES + part * capacity
                    out_ref[chip, :, lane : lane + capacity] = rows[t : t + 1, :]


def pack(positions, forces, rest_length, moduli, rest_bend, devices):
    operands = (positions, forces, rest_length, moduli, rest_bend)
    nodes = positions.shape[1]
    return pl.pallas_call(
        pack_kernel,
        out_shape=jax.ShapeDtypeStruct((devices // 2, 1, 6 * nodes + 2 * FOLD * LANES), jnp.float32),
        in_specs=[pl.BlockSpec(memory_space=pl.ANY)] * 5,
        out_specs=VMEM,
        scratch_shapes=[pltpu.VMEM(x.shape, x.dtype) for x in operands]
        + [pltpu.VMEM((PARAMS, rest_length.shape[1]), jnp.float32), pltpu.SemaphoreType.DMA((5,))],
        compiler_params=pltpu.CompilerParams(vmem_limit_bytes=60 * 1024 * 1024),
    )(*operands)


def pick_slots(capacity, near_ref, far_ref, owner_ref, params_ref):
    chips = near_ref.shape[0]
    nodes = owner_ref.shape[1]
    parts = PARAMS // FOLD
    owner = owner_ref[...]
    across = jnp.broadcast_to(owner, (nodes, nodes))
    earlier = lax.broadcasted_iota(jnp.int32, (nodes, nodes), 0) < lax.broadcasted_iota(
        jnp.int32, (nodes, nodes), 1
    )
    rank = jnp.sum(jnp.where((across == across.T) & earlier, 1, 0), axis=0, keepdims=True)
    parity = lax.axis_index("src") & 1
    spots = range(0, nodes, LANES)
    part = jnp.minimum(lax.broadcasted_iota(jnp.int32, (ROWS, LANES), 0), parts - 1)
    places = [rank[:, at : at + LANES] + part * capacity for at in spots]
    owners = [jnp.broadcast_to(owner[:, at : at + LANES], (ROWS, LANES)) for at in spots]

    def choose(step, chosen):
        chosen = list(chosen)
        chips_now = [step * PICK_UNROLL + i for i in range(PICK_UNROLL)]
        pairs = [(near_ref, chip, 2 * chip + parity) for chip in chips_now]
        pairs += [(far_ref, chip, 2 * chip + 1 - parity) for chip in chips_now]
        for ref, chip, device in pairs:
            for t in range(FOLD):
                lane = pl.multiple_of(6 * nodes + (parity * FOLD + t) * LANES, LANES)
                block = jnp.broadcast_to(ref[chip, :, pl.ds(lane, LANES)], (ROWS, LANES))
                for i in range(len(spots)):
                    taken = jnp.take_along_axis(block, places[i], axis=1, mode="promise_in_bounds")
                    at = i * FOLD + t
                    chosen[at] = jnp.where(owners[i] == device, taken, chosen[at])
        return tuple(chosen)

    zero = jnp.zeros((ROWS, LANES), jnp.float32)
    chosen = lax.fori_loop(0, chips // PICK_UNROLL, choose, (zero,) * (FOLD * len(spots)))
    for i, at in enumerate(spots):
        for t in range(FOLD):
            for j in range(parts):
                params_ref[j * FOLD + t : j * FOLD + t + 1, at : at + LANES] = chosen[i * FOLD + t][j : j + 1, :]


def spread_columns(own_ref, column_ref):
    nodes = column_ref.shape[1]
    for c in range(3):
        for at in range(0, nodes, LANES):
            row = own_ref[0, :, c * nodes + at : c * nodes + at + LANES]
            column_ref[c, at : at + LANES, :] = jnp.broadcast_to(row, (LANES, LANES)).T


def add_block(source_ref, nodes, device, at, target, totals):
    rows = [source_ref[device, :, c * nodes + at : c * nodes + at + LANES] for c in range(6)]
    x, f = rows[:3], rows[3:]
    d = [target[c] - x[c] for c in range(3)]
    shifted = d[0] * d[0] + (d[1] * d[1] + (d[2] * d[2] + 1.0))
    r = lax.rsqrt(shifted)
    cube = r * (r * r)
    direct = r + cube
    along = (d[0] * f[0] + d[1] * f[1] + d[2] * f[2]) * cube
    return tuple(totals[c] + (direct * f[c] + along * d[c]) for c in range(3))


def pair_sums(source_refs, column_ref, start_ref, sum_ref):
    nodes = column_ref.shape[1]

    def per_target(block, _):
        rows = pl.ds(pl.multiple_of(block * TARGET_ROWS, TARGET_ROWS), TARGET_ROWS)
        target = [column_ref[c, rows, :] for c in range(3)]
        if start_ref is None:
            totals = (jnp.zeros((TARGET_ROWS, LANES), jnp.float32),) * 3
        else:
            totals = tuple(start_ref[c, rows, :] for c in range(3))
        for source_ref in source_refs:
            together = math.gcd(source_ref.shape[0], UNROLL)

            def per_pass(step, totals):
                for i in range(together):
                    for at in range(0, nodes, LANES):
                        totals = add_block(source_ref, nodes, step * together + i, at, target, totals)
                return totals

            totals = lax.fori_loop(0, source_ref.shape[0] // together, per_pass, totals)
        for c in range(3):
            sum_ref[c, rows, :] = totals[c]
        return 0

    lax.fori_loop(0, nodes // TARGET_ROWS, per_target, 0)


def velocity_rows(sum_ref, scale):
    nodes = sum_ref.shape[1]
    velocity = []
    for c in range(3):
        parts = [
            jnp.sum(sum_ref[c, at : at + LANES, :].T, axis=0, keepdims=True)
            for at in range(0, nodes, LANES)
        ]
        velocity.append(jnp.concatenate(parts, axis=1) * (inverse_blob * scale))
    return velocity


def membrane(x, neighbours_ref, params_ref):
    nodes = x[0].shape[1]
    force = [[], [], []]
    for at in range(0, nodes, LANES):
        here = slice(at, at + LANES)
        points = [neighbours_ref[0:6, here], neighbours_ref[6:12, here]]
        edges = []
        for index in points:
            local = index & (LANES - 1)
            group = index // LANES
            component = []
            for c in range(3):
                found = jnp.zeros(index.shape, jnp.float32)
                for part in range(nodes // LANES):
                    source = jnp.broadcast_to(x[c][:, part * LANES : (part + 1) * LANES], index.shape)
                    taken = jnp.take_along_axis(source, local, axis=1, mode="promise_in_bounds")
                    found = jnp.where(group == part, taken, found)
                component.append(found - x[c][:, here])
            edges.append(component)
        near, far = edges
        length = params_ref[0:6, here]
        stretch = (near[0] * near[0] + near[1] * near[1] + near[2] * near[2]) / (length * length)
        tension = (stretch - 1.0) / (stretch + 1.0) / length
        for c in range(3):
            surface = jnp.sum(tension * near[c], axis=0, keepdims=True)
            bending = jnp.sum((2.0 / 9.0) * near[c] - (1.0 / 18.0) * far[c], axis=0, keepdims=True)
            bending = bending - params_ref[8 + c : 9 + c, here]
            force[c].append(params_ref[6:7, here] * surface + params_ref[7:8, here] * bending)
    return [jnp.concatenate(parts, axis=1) for parts in force]


def near_kernel(source_ref, own_ref, column_ref, sum_ref):
    spread_columns(own_ref, column_ref)
    pair_sums([source_ref], column_ref, None, sum_ref)


def advance(scale, position_ref, sum_ref, neighbours_ref, params_ref, out_ref, moved_ref):
    velocity = velocity_rows(sum_ref, scale)
    nodes = velocity[0].shape[1]
    x = [position_ref[c : c + 1, :] + time_step * velocity[c] for c in range(3)]
    for c in range(3):
        moved_ref[c : c + 1, :] = x[c]
    scaled = [inverse_blob * v for v in x]
    force = membrane(x, neighbours_ref, params_ref)
    for chip in range(out_ref.shape[0]):
        for c in range(3):
            out_ref[chip, :, c * nodes : (c + 1) * nodes] = scaled[c]
            out_ref[chip, :, (3 + c) * nodes : (4 + c) * nodes] = force[c]


def first_kernel(scale, capacity, *refs):
    far_ref, position_ref, column_ref, start_ref, neighbours_ref, near_ref, owner_ref = refs[:7]
    out_ref, moved_ref, params_ref, sum_ref = refs[7:]
    pick_slots(capacity, near_ref, far_ref, owner_ref, params_ref)
    pair_sums([far_ref], column_ref, start_ref, sum_ref)
    advance(scale, position_ref, sum_ref, neighbours_ref, params_ref, out_ref, moved_ref)


def step_kernel(scale, *refs):
    far_ref, position_ref, column_ref, start_ref, neighbours_ref, params_ref, out_ref, moved_ref, sum_ref = refs
    pair_sums([far_ref], column_ref, start_ref, sum_ref)
    advance(scale, position_ref, sum_ref, neighbours_ref, params_ref, out_ref, moved_ref)


def last_kernel(scale, far_ref, column_ref, start_ref, velocity_ref, sum_ref):
    pair_sums([far_ref], column_ref, start_ref, sum_ref)
    velocity = velocity_rows(sum_ref, scale)
    for c in range(3):
        velocity_ref[c : c + 1, :] = velocity[c]


def spread(copies, devices):
    parities = [list(range(parity, devices, 2)) for parity in range(2)]
    near = lax.all_to_all(copies, AXES, split_axis=0, concat_axis=0, axis_index_groups=parities, tiled=True)
    far = lax.ppermute(near, AXES, [(i, i ^ 1) for i in range(devices)])
    return near, far


def near_sums(near, copies, nodes):
    shape = jax.ShapeDtypeStruct((3, nodes, LANES), jnp.float32)
    pairs = near.shape[0] * nodes * nodes
    return pl.pallas_call(
        near_kernel,
        out_shape=(shape, shape),
        in_specs=[VMEM] * 2,
        out_specs=(VMEM,) * 2,
        compiler_params=GRANT,
        cost_estimate=pl.CostEstimate(flops=31 * pairs, bytes_accessed=8 * 3 * nodes * LANES, transcendentals=pairs),
    )(near, copies)


def call(kernel, out_shape, operands, nodes):
    return pl.pallas_call(
        kernel,
        out_shape=out_shape,
        in_specs=[VMEM] * len(operands),
        out_specs=jax.tree.map(lambda _: VMEM, out_shape),
        scratch_shapes=[pltpu.VMEM((3, nodes, LANES), jnp.float32)],
        compiler_params=GRANT,
    )(*operands)


def body(positions, forces, neighbours, patch_owner, rest_length, moduli, rest_bend):
    devices = lax.axis_size("tgt") * lax.axis_size("src")
    nodes = positions.shape[1]
    scale = 1.0 / math.sqrt(devices * nodes)
    capacity = rest_length.shape[1] // devices
    copies_shape = jax.ShapeDtypeStruct((devices // 2, 1, 6 * nodes), jnp.float32)
    params_shape = jax.ShapeDtypeStruct((PARAMS, nodes), jnp.float32)
    row_shape = jax.ShapeDtypeStruct((3, nodes), jnp.float32)
    position = positions
    copies = pack(positions, forces, rest_length, moduli, rest_bend, devices)
    for step in range(STEPS + 1):
        near, far = spread(copies, devices)
        column, start = near_sums(near, copies, nodes)
        operands = (far, position, column, start)
        if step == 0:
            copies, position, params = call(
                functools.partial(first_kernel, scale, capacity),
                (copies_shape, row_shape, params_shape),
                operands + (neighbours, near, patch_owner.reshape(1, nodes)),
                nodes,
            )
        elif step < STEPS:
            operands = operands + (neighbours, params)
            shapes = (copies_shape, row_shape)
            copies, position = call(functools.partial(step_kernel, scale), shapes, operands, nodes)
    velocity = call(functools.partial(last_kernel, scale), row_shape, (far, column, start), nodes)
    return position, velocity


def solution(mesh):
    placed = (
        P(None, AXES),
        P(None, AXES),
        P(None, AXES),
        P(AXES, None),
        P(None, AXES),
        P(None, AXES),
        P(None, AXES),
    )
    return jax.shard_map(
        body,
        mesh=mesh,
        in_specs=placed,
        out_specs=(P(None, AXES), P(None, AXES)),
        check_vma=False,
    )
```

```python
import functools
import math

import jax
import jax.numpy as jnp
import numpy as np
from jax import lax
from jax.experimental import pallas as pl
from jax.experimental.pallas import tpu as pltpu
from jax.sharding import Mesh
from jax.sharding import PartitionSpec as P

STEPS = 3
LANES = 128
ROWS = 8
PIECES = 32
DEPTH = 128
FAR_OFF = 2048.0
CUT_UNROLL = 4
CHUNK = 16
LOADS = 7
SIDE = 32
PICK_UNROLL = 4
PARAMS = 12
FOLD = 4

inverse_blob = 20.0
time_step = 0.5

CHIPS = ("tgt", "z")
AXES = CHIPS + ("core",)
VMEM = pl.BlockSpec(memory_space=pltpu.VMEM)
GRANT = pltpu.CompilerParams(vmem_limit_bytes=32 * 1024 * 1024)


def pack_kernel(*refs):
    inputs, (out_ref, side_ref), copies = refs[:LOADS], refs[LOADS : LOADS + 2], refs[LOADS + 2 : -3]
    slots_ref, target_ref, semaphores = refs[-3:]
    loads = [pltpu.make_async_copy(inputs[i], copies[i], semaphores.at[i]) for i in range(LOADS)]
    for load in loads:
        load.start()
    for load in loads:
        load.wait()
    position_ref, force_ref, length_ref, moduli_ref, bend_ref, owner_ref, select_ref = copies
    chips = out_ref.shape[0]
    nodes = position_ref.shape[1]
    capacity = length_ref.shape[1] // (2 * chips)
    state = [inverse_blob * position_ref[c : c + 1, :] for c in range(3)]
    make_left(state, select_ref, side_ref, target_ref)
    rank_nodes(owner_ref, side_ref)
    state += [force_ref[c : c + 1, :] for c in range(3)]
    slots_ref[0:6, :] = length_ref[...]
    slots_ref[6:8, :] = moduli_ref[...]
    slots_ref[8:11, :] = bend_ref[...]
    slots_ref[11:12, :] = bend_ref[0:1, :]
    for chip in range(chips):
        for c in range(6):
            out_ref[chip, :, c * nodes : (c + 1) * nodes] = state[c]
        for core in range(2):
            cut = slice((2 * chip + core) * capacity, (2 * chip + core + 1) * capacity)
            for part in range(PARAMS // FOLD):
                rows = slots_ref[part * FOLD : (part + 1) * FOLD, cut]
                for t in range(FOLD):
                    lane = 6 * nodes + (core * FOLD + t) * LANES + part * capacity
                    out_ref[chip, :, lane : lane + capacity] = rows[t : t + 1, :]


def side_shape(nodes):
    return jax.ShapeDtypeStruct((2 * nodes + SIDE, DEPTH), jnp.float32)


def pack(positions, forces, rest_length, moduli, rest_bend, owner, select, devices):
    operands = (positions, forces, rest_length, moduli, rest_bend, owner, select)
    nodes = positions.shape[1]
    return pl.pallas_call(
        pack_kernel,
        out_shape=(
            jax.ShapeDtypeStruct((devices // 2, 1, 6 * nodes + 2 * FOLD * LANES), jnp.float32),
            side_shape(nodes),
        ),
        in_specs=[pl.BlockSpec(memory_space=pl.ANY)] * LOADS,
        out_specs=(VMEM,) * 2,
        scratch_shapes=[pltpu.VMEM(x.shape, x.dtype) for x in operands]
        + [
            pltpu.VMEM((PARAMS, rest_length.shape[1]), jnp.float32),
            pltpu.VMEM((PIECES, nodes), jnp.float32),
            pltpu.SemaphoreType.DMA((LOADS,)),
        ],
        compiler_params=pltpu.CompilerParams(vmem_limit_bytes=60 * 1024 * 1024),
    )(*operands)


def rank_nodes(owner_ref, side_ref):
    nodes = owner_ref.shape[1]
    owner = owner_ref[...]
    across = jnp.broadcast_to(owner, (nodes, nodes))
    earlier = lax.broadcasted_iota(jnp.int32, (nodes, nodes), 0) < lax.broadcasted_iota(
        jnp.int32, (nodes, nodes), 1
    )
    rank = jnp.sum(jnp.where((across == across.T) & earlier, 1, 0), axis=0, keepdims=True)
    first = side_ref.shape[0] - ROWS
    for v in (rank, owner):
        for at in range(0, nodes, LANES):
            side_ref[first : first + 1, :] = v[:, at : at + LANES].astype(jnp.float32)
            first += 1


def pick_slots(capacity, near_ref, far_ref, side_ref, params_ref):
    chips = near_ref.shape[0]
    nodes = params_ref.shape[1]
    parts = PARAMS // FOLD
    named = side_ref[side_ref.shape[0] - ROWS :, :].astype(jnp.int32)
    parity = lax.axis_index("core")
    spots = range(0, nodes, LANES)
    part = jnp.minimum(lax.broadcasted_iota(jnp.int32, (ROWS, LANES), 0), parts - 1)
    places = [named[i : i + 1, :] + part * capacity for i in range(len(spots))]
    owners = [jnp.broadcast_to(named[len(spots) + i : len(spots) + i + 1, :], (ROWS, LANES)) for i in range(len(spots))]

    def choose(step, chosen):
        chosen = list(chosen)
        chips_now = [step * PICK_UNROLL + i for i in range(PICK_UNROLL)]
        pairs = [(near_ref, chip, 2 * chip + parity) for chip in chips_now]
        pairs += [(far_ref, chip, 2 * chip + 1 - parity) for chip in chips_now]
        for ref, chip, device in pairs:
            for t in range(FOLD):
                lane = pl.multiple_of(6 * nodes + (parity * FOLD + t) * LANES, LANES)
                block = jnp.broadcast_to(ref[chip, :, pl.ds(lane, LANES)], (ROWS, LANES))
                for i in range(len(spots)):
                    taken = jnp.take_along_axis(block, places[i], axis=1, mode="promise_in_bounds")
                    at = i * FOLD + t
                    chosen[at] = jnp.where(owners[i] == device, taken, chosen[at])
        return tuple(chosen)

    zero = jnp.zeros((ROWS, LANES), jnp.float32)
    chosen = lax.fori_loop(0, chips // PICK_UNROLL, choose, (zero,) * (FOLD * len(spots)))
    for i, at in enumerate(spots):
        for t in range(FOLD):
            for j in range(parts):
                params_ref[j * FOLD + t : j * FOLD + t + 1, at : at + LANES] = chosen[i * FOLD + t][j : j + 1, :]


def high(v):
    return v.astype(jnp.bfloat16).astype(jnp.float32)


def three(v):
    first = high(v)
    second = high(v - first)
    return first, second, (v - first) - second


def on_grid(v, grid, per_grid):
    return jnp.floor(v * per_grid + 0.5) * grid


def norm_and_cross(x, coarse):
    rest = [v - w for v, w in zip(x, coarse)]
    norm = coarse[0] * coarse[0] + coarse[1] * coarse[1] + coarse[2] * coarse[2]
    cross = [(2.0 * w + r) * r for w, r in zip(coarse, rest)]
    return norm, cross[0] + cross[1] + cross[2]


def selectors():
    c1, c2, r1, r2, n, g, one = 0, 3, 6, 9, 12, 15, 18
    A,B,C,D,E,F,G,H = range(0,128,16)
    s = np.zeros((PIECES, DEPTH), np.float32); t = np.zeros((PIECES, DEPTH), np.float32)
    for at, first in ((A,c1),(B,c2),(C,c1),(D,c2),(E,r1),(F,r2),(G,r1),(H,r2)):
        for c in range(3):
            s[first+c, at+c] = -2.0
            s[first+c, at+8+c] = -2.0
    s[one, A+6] = s[one, A+14] = s[one, A+15] = 1.0
    s[n, A+7] = s[n+1, B+7] = s[n+2, E+7] = 1.0
    s[one, C+6] = s[one, C+14] = s[one, C+15] = 1.0
    s[g, C+7] = s[g+1, D+7] = s[g+2, G+7] = 1.0
    for at, first, second in ((A,c1,c1),(B,c2,c2),(C,c1,None),(D,c2,None),(E,r1,r1),(F,r2,None)):
        for c in range(3):
            t[first+c, at+3+c] = 1.0
            if second is not None: t[second+c, at+11+c] = 1.0
    for c in range(3): t[one, C+11+c] = 1.0
    return np.concatenate([s, t], axis=1)


def own_rows(own_ref, nodes):
    return [own_ref[0, :, c * nodes : (c + 1) * nodes] for c in range(3)]


def pick_grid(size):
    grid = jnp.full(size.shape, 2.0**-3, jnp.float32)
    per_grid = jnp.full(size.shape, 2.0**3, jnp.float32)
    for step in range(1, 25):
        beyond = size > 2.0 ** (6 + step)
        grid = jnp.where(beyond, 2.0 ** (step - 3), grid)
        per_grid = jnp.where(beyond, 2.0 ** (3 - step), per_grid)
    return grid, per_grid


def set_grid(size, info_ref):
    grid, per_grid = pick_grid(size)
    info_ref[0:ROWS, :] = jnp.broadcast_to(grid, (ROWS, LANES))
    info_ref[ROWS : 2 * ROWS, :] = jnp.broadcast_to(per_grid, (ROWS, LANES))


def build_left(x, select_ref, info_ref, target_ref, left_ref):
    grid, per_grid = info_ref[0:1, 0:1], info_ref[ROWS : ROWS + 1, 0:1]
    shift = [info_ref[2 * ROWS + c : 2 * ROWS + c + 1, 0:1] for c in range(3)]
    x = [v - o for v, o in zip(x, shift)]
    coarse = [on_grid(v, grid, per_grid) for v in x]
    norm, cross = norm_and_cross(x, coarse)
    c1 = [high(v) for v in coarse]
    r1 = [high(v - w) for v, w in zip(x, coarse)]
    pieces = c1 + [v - w for v, w in zip(coarse, c1)]
    pieces += r1 + [(v - w) - r for v, w, r in zip(x, coarse, r1)]
    pieces += list(three(norm)) + list(three(cross + 1.0)) + [jnp.ones_like(norm)]
    target_ref[...] = jnp.zeros(target_ref.shape, jnp.float32)
    for r, piece in enumerate(pieces):
        target_ref[r : r + 1, :] = piece
    left = lax.dot_general(
        target_ref[...].astype(jnp.bfloat16),
        select_ref[...].astype(jnp.bfloat16),
        (((0,), (0,)), ((), ())),
        preferred_element_type=jnp.float32,
    ).astype(jnp.bfloat16)
    nodes = left.shape[0]
    left_ref[0:nodes, :] = left[:, 0:DEPTH].astype(left_ref.dtype)
    left_ref[nodes : 2 * nodes, :] = left[:, DEPTH : 2 * DEPTH].astype(left_ref.dtype)


def info_of(side_ref):
    rows = side_ref.shape[0] - SIDE
    return side_ref.at[rows : rows + 3 * ROWS, :]


def make_left(x, select_ref, side_ref, target_ref):
    info_ref = info_of(side_ref)
    size = jnp.max(functools.reduce(jnp.maximum, [jnp.abs(v) for v in x]), axis=1, keepdims=True)
    shift = [jnp.where(size > FAR_OFF, v[:, 0:1], 0.0) for v in x]
    info_ref[2 * ROWS : 3 * ROWS, :] = jnp.zeros((ROWS, LANES), jnp.float32)
    for c in range(3):
        info_ref[2 * ROWS + c : 2 * ROWS + c + 1, :] = jnp.broadcast_to(shift[c], (1, LANES))
    apart = functools.reduce(jnp.maximum, [jnp.abs(v - o) for v, o in zip(x, shift)])
    set_grid(2.0 * jnp.max(apart, axis=1, keepdims=True), info_ref)
    build_left(x, select_ref, info_ref, target_ref, side_ref)


def cut_sources(source_ref, own_ref, select_ref, side_ref, work):
    pieces_ref, row_ref, target_ref, my_left_ref, my_info_ref = work[:5]
    halves = pieces_ref.shape[0]
    blocks = pieces_ref.shape[1] // PIECES
    stride = source_ref.shape[0] // blocks
    info_ref = info_of(side_ref)
    my_left_ref[...] = side_ref[0 : my_left_ref.shape[0], :].astype(jnp.bfloat16)
    my_info_ref[...] = info_ref[...]
    shift = [info_ref[2 * ROWS + c : 2 * ROWS + c + 1, :] for c in range(3)]
    x, f = [], []
    for h in range(halves):
        rows = [source_ref[pl.ds(c * halves + h, blocks, stride=stride), :] for c in range(6)]
        x.append([rows[c] - shift[c] for c in range(3)])
        f.append(rows[3:])
    size = functools.reduce(jnp.maximum, [jnp.abs(v) for part in x for v in part])
    size = jnp.max(jnp.max(size, axis=0, keepdims=True), axis=1, keepdims=True)
    beyond = jnp.max(size - 1024.0 * info_ref[0:1, 0:1]) > 0.0

    @pl.when(beyond)
    def _():
        set_grid(size, my_info_ref)
        build_left(own_rows(own_ref, target_ref.shape[1]), select_ref, my_info_ref, target_ref, my_left_ref)

    grid, per_grid = my_info_ref[0:1, :], my_info_ref[ROWS : ROWS + 1, :]
    for h in range(halves):
        norm, cross = norm_and_cross(x[h], [on_grid(v, grid, per_grid) for v in x[h]])
        n, g = three(norm), three(cross)
        c = three(-(x[h][0] * f[h][0] + x[h][1] * f[h][1] + x[h][2] * f[h][2]))
        one = jnp.ones_like(norm)
        sums = ((6, n[0]), (7, one), (14, n[1]), (15, n[2]), (22, g[0]), (23, one))
        sums += ((27, c[0]), (28, c[1]), (29, c[2]), (30, g[1]), (31, g[2]))
        for r, v in sums:
            pieces_ref[h, pl.ds(r, blocks, stride=PIECES), :] = v
    grid, per_grid = my_info_ref[0:6, :], my_info_ref[ROWS : ROWS + 6, :]
    shifts = my_info_ref[2 * ROWS : 2 * ROWS + 6, :]
    is_x = lax.broadcasted_iota(jnp.int32, (6, LANES), 0) < 3

    def cut(step, _):
        for i in range(CUT_UNROLL):
            block = step * CUT_UNROLL + i
            at = pl.multiple_of(block * PIECES, PIECES)
            for h in range(halves):
                tile = source_ref[pl.ds(block * stride + h, 6, stride=halves), :] - shifts
                coarse = on_grid(tile, grid, per_grid)
                rest = tile - coarse
                c1, r1, f1 = high(coarse), high(rest), high(tile)
                left_over = tile - f1
                f2 = high(left_over)
                pieces_ref[h, pl.ds(at, 6), :] = jnp.where(is_x, c1, f1)
                pieces_ref[h, pl.ds(at + 8, 6), :] = jnp.where(is_x, coarse - c1, f2)
                pieces_ref[h, pl.ds(at + 16, 6), :] = jnp.where(is_x, r1, left_over - f2)
                pieces_ref[h, pl.ds(at + 24, 3), :] = (rest - r1)[0:3]
                row_ref[h, pl.ds(pl.multiple_of(block * ROWS, ROWS), 6), :] = tile
        return 0

    lax.fori_loop(0, blocks // CUT_UNROLL, cut, 0)


def pair_sums(source_ref, own_ref, select_ref, side_ref, start_ref, sum_ref, work):
    pieces_ref, row_ref, _, my_left_ref, _, *product_refs = work
    nodes = sum_ref.shape[1]
    halves = pieces_ref.shape[0]
    blocks = pieces_ref.shape[1] // PIECES
    cut_sources(source_ref, own_ref, select_ref, side_ref, work)
    looped = blocks > CHUNK
    if looped:
        sum_ref[...] = jnp.zeros(sum_ref.shape, jnp.float32) if start_ref is None else start_ref[...]

    def multiply(first, into):
        for i, product_ref in enumerate(into):
            here = pl.ds(pl.multiple_of((first + i) * PIECES, PIECES), PIECES)
            rows = jnp.concatenate([pieces_ref[h, here, :] for h in range(halves)], axis=1).astype(jnp.bfloat16)
            p, q = rows[0:16], rows[16:32]
            right = jnp.concatenate([p, p, q, q, p, p, q, q], axis=0)
            for kind in range(2):
                product_ref[kind] = jnp.dot(
                    my_left_ref[kind * nodes : (kind + 1) * nodes, :], right, preferred_element_type=jnp.float32
                )

    def add(first, ready, fresh=False):
        tiles = []
        for i, product_ref in enumerate(ready):
            here = pl.ds(pl.multiple_of((first + i) * ROWS, ROWS), ROWS)
            for h in range(halves):
                lanes = slice(h * LANES, (h + 1) * LANES)
                rows = row_ref[h, here, :]
                spread = [jnp.broadcast_to(rows[r : r + 1, :], (ROWS, LANES)) for r in range(6)]
                tiles.append((product_ref, lanes, spread))
        for at in range(0, nodes, ROWS):
            here = slice(at, at + ROWS)
            if fresh and start_ref is None:
                totals = [jnp.zeros((ROWS, LANES), jnp.float32)] * 4
            else:
                totals = [(start_ref if fresh else sum_ref)[c, here, :] for c in range(4)]
            for product_ref, lanes, spread in tiles:
                r = lax.rsqrt(jnp.maximum(product_ref[0, here, lanes], 1.0))
                cube = r * (r * r)
                direct = r + cube
                along = product_ref[1, here, lanes] * cube
                for c in range(3):
                    totals[c] = totals[c] + (direct * spread[3 + c] - along * spread[c])
                totals[3] = totals[3] + along
            for c in range(4):
                sum_ref[c, here, :] = totals[c]

    def chunk(first, count):
        multiply(first, product_refs[0:2])
        for i in range(0, count, 4):
            multiply(first + i + 2, product_refs[2:4])
            add(first + i, product_refs[0:2], fresh=i == 0 and not looped)
            if i + 4 < count:
                multiply(first + i + 4, product_refs[0:2])
            add(first + i + 2, product_refs[2:4])

    if not looped:
        chunk(0, blocks)
    else:

        def step(i, _):
            chunk(i * CHUNK, CHUNK)
            return 0

        lax.fori_loop(0, blocks // CHUNK, step, 0)


def velocity_rows(own_ref, info_ref, sum_ref, scale):
    nodes = sum_ref.shape[1]
    sums = []
    for c in range(4):
        parts = [
            jnp.sum(sum_ref[c, at : at + LANES, :].T, axis=0, keepdims=True)
            for at in range(0, nodes, LANES)
        ]
        sums.append(jnp.concatenate(parts, axis=1))
    shift = [info_ref[2 * ROWS + c : 2 * ROWS + c + 1, 0:1] for c in range(3)]
    x = [v - o for v, o in zip(own_rows(own_ref, nodes), shift)]
    return [(sums[c] + x[c] * sums[3]) * (inverse_blob * scale) for c in range(3)]


def membrane(x, neighbours_ref, params_ref):
    nodes = x[0].shape[1]
    force = [[], [], []]
    for at in range(0, nodes, LANES):
        here = slice(at, at + LANES)
        points = [neighbours_ref[0:6, here], neighbours_ref[6:12, here]]
        edges = []
        for index in points:
            local = index & (LANES - 1)
            group = index // LANES
            component = []
            for c in range(3):
                found = jnp.zeros(index.shape, jnp.float32)
                for part in range(nodes // LANES):
                    source = jnp.broadcast_to(x[c][:, part * LANES : (part + 1) * LANES], index.shape)
                    taken = jnp.take_along_axis(source, local, axis=1, mode="promise_in_bounds")
                    found = jnp.where(group == part, taken, found)
                component.append(found - x[c][:, here])
            edges.append(component)
        near, far = edges
        length = params_ref[0:6, here]
        stretch = (near[0] * near[0] + near[1] * near[1] + near[2] * near[2]) / (length * length)
        tension = (stretch - 1.0) / (stretch + 1.0) / length
        for c in range(3):
            surface = jnp.sum(tension * near[c], axis=0, keepdims=True)
            bending = jnp.sum((2.0 / 9.0) * near[c] - (1.0 / 18.0) * far[c], axis=0, keepdims=True)
            bending = bending - params_ref[8 + c : 9 + c, here]
            force[c].append(params_ref[6:7, here] * surface + params_ref[7:8, here] * bending)
    return [jnp.concatenate(parts, axis=1) for parts in force]


def near_kernel(source_ref, own_ref, select_ref, side_ref, sum_ref, *work):
    pair_sums(source_ref, own_ref, select_ref, side_ref, None, sum_ref, work)


def advance(scale, sources, work, position_ref, sum_ref, neighbours_ref, params_ref, outs):
    out_ref, moved_ref, next_side_ref = outs
    own_ref, select_ref, side_ref = sources[1:4]
    velocity = velocity_rows(own_ref, info_of(side_ref), sum_ref, scale)
    nodes = velocity[0].shape[1]
    x = [position_ref[c : c + 1, :] + time_step * velocity[c] for c in range(3)]
    for c in range(3):
        moved_ref[c : c + 1, :] = x[c]
    scaled = [inverse_blob * v for v in x]
    force = membrane(x, neighbours_ref, params_ref)
    make_left(scaled, select_ref, next_side_ref, work[2])
    for chip in range(out_ref.shape[0]):
        for c in range(3):
            out_ref[chip, :, c * nodes : (c + 1) * nodes] = scaled[c]
            out_ref[chip, :, (3 + c) * nodes : (4 + c) * nodes] = force[c]


def first_kernel(scale, capacity, *refs):
    *sources, start_ref, position_ref, neighbours_ref, near_ref, far_ref = refs[:9]
    outs, (params_ref, sum_ref, *work) = refs[9:12], refs[12:]
    pick_slots(capacity, near_ref, far_ref, sources[3], params_ref)
    pair_sums(*sources, start_ref, sum_ref, work)
    advance(scale, sources, work, position_ref, sum_ref, neighbours_ref, params_ref, outs)


def step_kernel(scale, *refs):
    *sources, start_ref, position_ref, neighbours_ref, params_ref = refs[:8]
    outs, (sum_ref, *work) = refs[8:11], refs[11:]
    pair_sums(*sources, start_ref, sum_ref, work)
    advance(scale, sources, work, position_ref, sum_ref, neighbours_ref, params_ref, outs)


def last_kernel(scale, *refs):
    *sources, start_ref, velocity_ref, sum_ref = refs[:7]
    pair_sums(*sources, start_ref, sum_ref, refs[7:])
    velocity = velocity_rows(sources[1], info_of(sources[3]), sum_ref, scale)
    for c in range(3):
        velocity_ref[c : c + 1, :] = velocity[c]


def spread(copies):
    near = lax.all_to_all(copies, CHIPS, split_axis=0, concat_axis=0, tiled=True)
    far = lax.ppermute(near, "core", [(0, 1), (1, 0)])
    return near, far


def call(kernel, out_shape, operands, blocks, nodes, keeps_sums):
    pairs = blocks * nodes * nodes
    sums = [] if keeps_sums else [pltpu.VMEM((4, nodes, LANES), jnp.float32)]
    return pl.pallas_call(
        kernel,
        out_shape=out_shape,
        in_specs=[VMEM] * len(operands),
        out_specs=jax.tree.map(lambda _: VMEM, out_shape),
        scratch_shapes=sums
        + [
            pltpu.VMEM((nodes // LANES, blocks * PIECES, LANES), jnp.float32),
            pltpu.VMEM((nodes // LANES, blocks * ROWS, LANES), jnp.float32),
            pltpu.VMEM((PIECES, nodes), jnp.float32),
            pltpu.VMEM((2 * nodes, DEPTH), jnp.bfloat16),
            pltpu.VMEM((3 * ROWS, LANES), jnp.float32),
        ]
        + [pltpu.VMEM((2, nodes, nodes), jnp.float32)] * 4,
        compiler_params=GRANT,
        cost_estimate=pl.CostEstimate(flops=31 * pairs, bytes_accessed=8 * 3 * nodes * LANES, transcendentals=pairs),
    )(*operands)


def body(positions, forces, neighbours, patch_owner, rest_length, moduli, rest_bend):
    devices = lax.axis_size(AXES)
    nodes = positions.shape[1]
    chips = devices // 2
    scale = 1.0 / math.sqrt(devices * nodes)
    capacity = rest_length.shape[1] // devices
    copies_shape = jax.ShapeDtypeStruct((chips, 1, 6 * nodes), jnp.float32)
    params_shape = jax.ShapeDtypeStruct((PARAMS, nodes), jnp.float32)
    row_shape = jax.ShapeDtypeStruct((3, nodes), jnp.float32)
    step_shapes = (copies_shape, row_shape, side_shape(nodes))
    sums_shape = jax.ShapeDtypeStruct((4, nodes, LANES), jnp.float32)
    select = jnp.asarray(selectors())
    position = positions
    owner = patch_owner.reshape(1, nodes)
    copies, side = pack(
        positions, forces, rest_length, moduli, rest_bend, owner, select, devices
    )
    for step in range(STEPS + 1):
        near, far = spread(copies)
        shared = (copies, select, side)
        start = call(near_kernel, sums_shape, (near.reshape(-1, LANES),) + shared, chips, nodes, True)
        operands = (far.reshape(-1, LANES),) + shared + (start,)
        if step == 0:
            operands += (position, neighbours, near, far)
            kernel = functools.partial(first_kernel, scale, capacity)
            shapes = (*step_shapes, params_shape)
            copies, position, side, params = call(kernel, shapes, operands, chips, nodes, False)
        elif step < STEPS:
            operands += (position, neighbours, params)
            kernel = functools.partial(step_kernel, scale)
            copies, position, side = call(kernel, step_shapes, operands, chips, nodes, False)
    velocity = call(functools.partial(last_kernel, scale), row_shape, operands, chips, nodes, False)
    return position, velocity


def solution(mesh):
    tgt, src = mesh.devices.shape
    by_core = Mesh(mesh.devices.reshape(tgt, src // 2, 2), AXES)
    placed = (
        P(None, AXES),
        P(None, AXES),
        P(None, AXES),
        P(AXES, None),
        P(None, AXES),
        P(None, AXES),
        P(None, AXES),
    )
    return jax.shard_map(
        body,
        mesh=by_core,
        in_specs=placed,
        out_specs=(P(None, AXES), P(None, AXES)),
        check_vma=False,
    )
```

```python
import functools
import math

import jax
import jax.numpy as jnp
import numpy as np
from jax import lax
from jax.experimental import pallas as pl
from jax.experimental.pallas import tpu as pltpu
from jax.sharding import Mesh
from jax.sharding import PartitionSpec as P

STEPS = 3
LANES = 128
ROWS = 8
PIECES = 32
DEPTH = 128
FAR_OFF = 2048.0
CUT_UNROLL = 4
CHUNK = 16
LOADS = 7
SIDE = 128
PICK_UNROLL = 4
PARAMS = 12
FOLD = 4

inverse_blob = 20.0
time_step = 0.5

CHIPS = ("tgt", "z")
AXES = CHIPS + ("core",)
VMEM = pl.BlockSpec(memory_space=pltpu.VMEM)
GRANT = pltpu.CompilerParams(vmem_limit_bytes=32 * 1024 * 1024)


def pack_kernel(*refs):
    inputs, (out_ref, side_ref), copies = refs[:LOADS], refs[LOADS : LOADS + 2], refs[LOADS + 2 : -4]
    slots_ref, target_ref, info_ref, semaphores = refs[-4:]
    loads = [pltpu.make_async_copy(inputs[i], copies[i], semaphores.at[i]) for i in range(LOADS)]
    for load in loads:
        load.start()
    for load in loads:
        load.wait()
    position_ref, force_ref, length_ref, moduli_ref, bend_ref, owner_ref, select_ref = copies
    chips = out_ref.shape[0]
    nodes = position_ref.shape[1]
    capacity = length_ref.shape[1] // (2 * chips)
    state = [inverse_blob * position_ref[c : c + 1, :] for c in range(3)]
    make_left(state, select_ref[...].astype(jnp.bfloat16), side_ref, info_ref, target_ref)
    rank_nodes(owner_ref, side_ref)
    state += [force_ref[c : c + 1, :] for c in range(3)]
    slots_ref[0:6, :] = length_ref[...]
    slots_ref[6:8, :] = moduli_ref[...]
    slots_ref[8:11, :] = bend_ref[...]
    slots_ref[11:12, :] = bend_ref[0:1, :]
    for chip in range(chips):
        for c in range(6):
            out_ref[chip, :, c * nodes : (c + 1) * nodes] = state[c]
        for core in range(2):
            cut = slice((2 * chip + core) * capacity, (2 * chip + core + 1) * capacity)
            for part in range(PARAMS // FOLD):
                rows = slots_ref[part * FOLD : (part + 1) * FOLD, cut]
                for t in range(FOLD):
                    lane = 6 * nodes + (core * FOLD + t) * LANES + part * capacity
                    out_ref[chip, :, lane : lane + capacity] = rows[t : t + 1, :]


def side_shape(nodes):
    return jax.ShapeDtypeStruct((2 * nodes + SIDE, DEPTH), jnp.bfloat16)


def pack(positions, forces, rest_length, moduli, rest_bend, owner, select, devices):
    operands = (positions, forces, rest_length, moduli, rest_bend, owner, select)
    nodes = positions.shape[1]
    return pl.pallas_call(
        pack_kernel,
        out_shape=(
            jax.ShapeDtypeStruct((devices // 2, 1, 6 * nodes + 2 * FOLD * LANES), jnp.float32),
            side_shape(nodes),
        ),
        in_specs=[pl.BlockSpec(memory_space=pl.ANY)] * LOADS,
        out_specs=(VMEM,) * 2,
        scratch_shapes=[pltpu.VMEM(x.shape, x.dtype) for x in operands]
        + [
            pltpu.VMEM((PARAMS, rest_length.shape[1]), jnp.float32),
            pltpu.VMEM((PIECES, nodes), jnp.float32),
            pltpu.VMEM((3 * ROWS, LANES), jnp.float32),
            pltpu.SemaphoreType.DMA((LOADS,)),
        ],
        compiler_params=pltpu.CompilerParams(vmem_limit_bytes=60 * 1024 * 1024),
    )(*operands)


def rank_nodes(owner_ref, side_ref):
    nodes = owner_ref.shape[1]
    owner = owner_ref[...]
    across = jnp.broadcast_to(owner, (nodes, nodes))
    earlier = lax.broadcasted_iota(jnp.int32, (nodes, nodes), 0) < lax.broadcasted_iota(
        jnp.int32, (nodes, nodes), 1
    )
    rank = jnp.sum(jnp.where((across == across.T) & earlier, 1, 0), axis=0, keepdims=True)
    rows = [v[:, at : at + LANES].astype(jnp.float32) for v in (rank, owner) for at in range(0, nodes, LANES)]
    rows.append(jnp.zeros((16 - len(rows), LANES), jnp.float32))
    first = side_ref.shape[0] - SIDE + 48
    side_ref[first : first + 16, :] = jnp.concatenate(rows, axis=0).astype(jnp.bfloat16)


def pick_slots(capacity, near_ref, far_ref, side_ref, params_ref):
    chips = near_ref.shape[0]
    nodes = params_ref.shape[1]
    parts = PARAMS // FOLD
    first = side_ref.shape[0] - SIDE + 48
    named = side_ref[first : first + 16, :].astype(jnp.float32).astype(jnp.int32)
    parity = lax.axis_index("core")
    spots = range(0, nodes, LANES)
    part = jnp.minimum(lax.broadcasted_iota(jnp.int32, (ROWS, LANES), 0), parts - 1)
    places = [named[i : i + 1, :] + part * capacity for i in range(len(spots))]
    owners = [jnp.broadcast_to(named[len(spots) + i : len(spots) + i + 1, :], (ROWS, LANES)) for i in range(len(spots))]

    def choose(step, chosen):
        chosen = list(chosen)
        chips_now = [step * PICK_UNROLL + i for i in range(PICK_UNROLL)]
        pairs = [(near_ref, chip, 2 * chip + parity) for chip in chips_now]
        pairs += [(far_ref, chip, 2 * chip + 1 - parity) for chip in chips_now]
        for ref, chip, device in pairs:
            for t in range(FOLD):
                lane = pl.multiple_of(6 * nodes + (parity * FOLD + t) * LANES, LANES)
                block = jnp.broadcast_to(ref[chip, :, pl.ds(lane, LANES)], (ROWS, LANES))
                for i in range(len(spots)):
                    taken = jnp.take_along_axis(block, places[i], axis=1, mode="promise_in_bounds")
                    at = i * FOLD + t
                    chosen[at] = jnp.where(owners[i] == device, taken, chosen[at])
        return tuple(chosen)

    zero = jnp.zeros((ROWS, LANES), jnp.float32)
    chosen = lax.fori_loop(0, chips // PICK_UNROLL, choose, (zero,) * (FOLD * len(spots)))
    for i, at in enumerate(spots):
        for t in range(FOLD):
            for j in range(parts):
                params_ref[j * FOLD + t : j * FOLD + t + 1, at : at + LANES] = chosen[i * FOLD + t][j : j + 1, :]


def high(v):
    return v.astype(jnp.bfloat16).astype(jnp.float32)


def three(v):
    first = high(v)
    second = high(v - first)
    return first, second, (v - first) - second


def on_grid(v, grid, per_grid):
    return jnp.floor(v * per_grid + 0.5) * grid


def norm_and_cross(x, coarse):
    rest = [v - w for v, w in zip(x, coarse)]
    norm = coarse[0] * coarse[0] + coarse[1] * coarse[1] + coarse[2] * coarse[2]
    cross = [(2.0 * w + r) * r for w, r in zip(coarse, rest)]
    return norm, cross[0] + cross[1] + cross[2]


def selectors():
    c1, c2, r1, r2, n, g, one = 0, 3, 6, 9, 12, 15, 18
    A,B,C,D,E,F,G,H = range(0,128,16)
    s = np.zeros((PIECES, DEPTH), np.float32); t = np.zeros((PIECES, DEPTH), np.float32)
    for at, first in ((A,c1),(B,c2),(C,c1),(D,c2),(E,r1),(F,r2),(G,r1),(H,r2)):
        for c in range(3):
            s[first+c, at+c] = -2.0
            s[first+c, at+8+c] = -2.0
    s[one, A+6] = s[one, A+14] = s[one, A+15] = 1.0
    s[n, A+7] = s[n+1, B+7] = s[n+2, E+7] = 1.0
    s[one, C+6] = s[one, C+14] = s[one, C+15] = 1.0
    s[g, C+7] = s[g+1, D+7] = s[g+2, G+7] = 1.0
    for at, first, second in ((A,c1,c1),(B,c2,c2),(C,c1,None),(D,c2,None),(E,r1,r1),(F,r2,None)):
        for c in range(3):
            t[first+c, at+3+c] = 1.0
            if second is not None: t[second+c, at+11+c] = 1.0
    for c in range(3): t[one, C+11+c] = 1.0
    return np.concatenate([s, t], axis=1)


def own_rows(own_ref, nodes):
    return [own_ref[0, :, c * nodes : (c + 1) * nodes] for c in range(3)]


def pick_grid(size):
    grid = jnp.full(size.shape, 2.0**-3, jnp.float32)
    per_grid = jnp.full(size.shape, 2.0**3, jnp.float32)
    for step in range(1, 25):
        beyond = size > 2.0 ** (6 + step)
        grid = jnp.where(beyond, 2.0 ** (step - 3), grid)
        per_grid = jnp.where(beyond, 2.0 ** (3 - step), per_grid)
    return grid, per_grid


def set_grid(size, info_ref):
    grid, per_grid = pick_grid(size)
    info_ref[0:ROWS, :] = jnp.broadcast_to(grid, (ROWS, LANES))
    info_ref[ROWS : 2 * ROWS, :] = jnp.broadcast_to(per_grid, (ROWS, LANES))


def build_left(x, select, info_ref, target_ref, left_ref):
    grid, per_grid = info_ref[0:1, 0:1], info_ref[ROWS : ROWS + 1, 0:1]
    shift = [info_ref[2 * ROWS + c : 2 * ROWS + c + 1, 0:1] for c in range(3)]
    x = [v - o for v, o in zip(x, shift)]
    coarse = [on_grid(v, grid, per_grid) for v in x]
    norm, cross = norm_and_cross(x, coarse)
    c1 = [high(v) for v in coarse]
    r1 = [high(v - w) for v, w in zip(x, coarse)]
    pieces = c1 + [v - w for v, w in zip(coarse, c1)]
    pieces += r1 + [(v - w) - r for v, w, r in zip(x, coarse, r1)]
    pieces += list(three(norm)) + list(three(cross + 1.0)) + [jnp.ones_like(norm)]
    target_ref[...] = jnp.zeros(target_ref.shape, jnp.float32)
    for r, piece in enumerate(pieces):
        target_ref[r : r + 1, :] = piece
    left = lax.dot_general(
        target_ref[...].astype(jnp.bfloat16),
        select,
        (((0,), (0,)), ((), ())),
        preferred_element_type=jnp.float32,
    ).astype(jnp.bfloat16)
    nodes = left.shape[0]
    left_ref[0:nodes, :] = left[:, 0:DEPTH].astype(left_ref.dtype)
    left_ref[nodes : 2 * nodes, :] = left[:, DEPTH : 2 * DEPTH].astype(left_ref.dtype)


def select_of(side_ref):
    first = side_ref.shape[0] - 2 * PIECES
    return jnp.concatenate(
        [side_ref[first : first + PIECES, :], side_ref[first + PIECES : first + 2 * PIECES, :]], axis=1
    )


def make_left(x, select, side_ref, info_ref, target_ref):
    size = jnp.max(functools.reduce(jnp.maximum, [jnp.abs(v) for v in x]), axis=1, keepdims=True)
    shift = [jnp.where(size > FAR_OFF, v[:, 0:1], 0.0) for v in x]
    info_ref[2 * ROWS : 3 * ROWS, :] = jnp.zeros((ROWS, LANES), jnp.float32)
    for c in range(3):
        info_ref[2 * ROWS + c : 2 * ROWS + c + 1, :] = jnp.broadcast_to(shift[c], (1, LANES))
    apart = functools.reduce(jnp.maximum, [jnp.abs(v - o) for v, o in zip(x, shift)])
    set_grid(2.0 * jnp.max(apart, axis=1, keepdims=True), info_ref)
    build_left(x, select, info_ref, target_ref, side_ref)
    first = side_ref.shape[0] - SIDE
    side_ref[first : first + 16, :] = info_ref[0 : 2 * ROWS, :].astype(jnp.bfloat16)
    rows = [*three(info_ref[2 * ROWS : 3 * ROWS, :]), jnp.zeros((ROWS, LANES), jnp.float32)]
    side_ref[first + 16 : first + 48, :] = jnp.concatenate(rows, axis=0).astype(jnp.bfloat16)
    side_ref[first + 64 : first + 64 + PIECES, :] = select[:, 0:DEPTH]
    side_ref[first + 64 + PIECES : first + SIDE, :] = select[:, DEPTH : 2 * DEPTH]


def cut_sources(source_ref, own_ref, side_ref, work):
    pieces_ref, row_ref, target_ref, my_left_ref, my_info_ref = work[:5]
    halves = pieces_ref.shape[0]
    blocks = pieces_ref.shape[1] // PIECES
    stride = source_ref.shape[0] // blocks
    first = my_left_ref.shape[0]
    my_left_ref[...] = side_ref[0:first, :]
    my_info_ref[0 : 2 * ROWS, :] = side_ref[first : first + 16, :].astype(jnp.float32)
    rows = side_ref[first + 16 : first + 48, :].astype(jnp.float32)
    my_info_ref[2 * ROWS : 3 * ROWS, :] = (rows[0:8] + rows[8:16]) + rows[16:24]
    shift = [my_info_ref[2 * ROWS + c : 2 * ROWS + c + 1, :] for c in range(3)]
    x, f = [], []
    for h in range(halves):
        rows = [source_ref[pl.ds(c * halves + h, blocks, stride=stride), :] for c in range(6)]
        x.append([rows[c] - shift[c] for c in range(3)])
        f.append(rows[3:])
    size = functools.reduce(jnp.maximum, [jnp.abs(v) for part in x for v in part])
    size = jnp.max(jnp.max(size, axis=0, keepdims=True), axis=1, keepdims=True)
    beyond = jnp.max(size - 1024.0 * my_info_ref[0:1, 0:1]) > 0.0

    @pl.when(beyond)
    def _():
        set_grid(size, my_info_ref)
        build_left(own_rows(own_ref, target_ref.shape[1]), select_of(side_ref), my_info_ref, target_ref, my_left_ref)

    grid, per_grid = my_info_ref[0:1, :], my_info_ref[ROWS : ROWS + 1, :]
    for h in range(halves):
        norm, cross = norm_and_cross(x[h], [on_grid(v, grid, per_grid) for v in x[h]])
        n, g = three(norm), three(cross)
        c = three(-(x[h][0] * f[h][0] + x[h][1] * f[h][1] + x[h][2] * f[h][2]))
        one = jnp.ones_like(norm)
        sums = ((6, n[0]), (7, one), (14, n[1]), (15, n[2]), (22, g[0]), (23, one))
        sums += ((27, c[0]), (28, c[1]), (29, c[2]), (30, g[1]), (31, g[2]))
        for r, v in sums:
            pieces_ref[h, pl.ds(r, blocks, stride=PIECES), :] = v
    grid, per_grid = my_info_ref[0:6, :], my_info_ref[ROWS : ROWS + 6, :]
    shifts = my_info_ref[2 * ROWS : 2 * ROWS + 6, :]
    is_x = lax.broadcasted_iota(jnp.int32, (6, LANES), 0) < 3

    def cut(step, _):
        for i in range(CUT_UNROLL):
            block = step * CUT_UNROLL + i
            at = pl.multiple_of(block * PIECES, PIECES)
            for h in range(halves):
                tile = source_ref[pl.ds(block * stride + h, 6, stride=halves), :] - shifts
                coarse = on_grid(tile, grid, per_grid)
                rest = tile - coarse
                c1, r1, f1 = high(coarse), high(rest), high(tile)
                left_over = tile - f1
                f2 = high(left_over)
                pieces_ref[h, pl.ds(at, 6), :] = jnp.where(is_x, c1, f1)
                pieces_ref[h, pl.ds(at + 8, 6), :] = jnp.where(is_x, coarse - c1, f2)
                pieces_ref[h, pl.ds(at + 16, 6), :] = jnp.where(is_x, r1, left_over - f2)
                pieces_ref[h, pl.ds(at + 24, 3), :] = (rest - r1)[0:3]
                row_ref[h, pl.ds(pl.multiple_of(block * ROWS, ROWS), 6), :] = tile
        return 0

    lax.fori_loop(0, blocks // CUT_UNROLL, cut, 0)


def pair_sums(source_ref, own_ref, side_ref, start_ref, sum_ref, work):
    pieces_ref, row_ref, _, my_left_ref, _, *product_refs = work
    nodes = sum_ref.shape[1]
    halves = pieces_ref.shape[0]
    blocks = pieces_ref.shape[1] // PIECES
    cut_sources(source_ref, own_ref, side_ref, work)
    looped = blocks > CHUNK
    if looped:
        sum_ref[...] = jnp.zeros(sum_ref.shape, jnp.float32) if start_ref is None else start_ref[...]

    def multiply(first, into):
        for i, product_ref in enumerate(into):
            here = pl.ds(pl.multiple_of((first + i) * PIECES, PIECES), PIECES)
            rows = jnp.concatenate([pieces_ref[h, here, :] for h in range(halves)], axis=1).astype(jnp.bfloat16)
            p, q = rows[0:16], rows[16:32]
            right = jnp.concatenate([p, p, q, q, p, p, q, q], axis=0)
            for kind in range(2):
                product_ref[kind] = jnp.dot(
                    my_left_ref[kind * nodes : (kind + 1) * nodes, :], right, preferred_element_type=jnp.float32
                )

    def add(first, ready, fresh=False):
        tiles = []
        for i, product_ref in enumerate(ready):
            here = pl.ds(pl.multiple_of((first + i) * ROWS, ROWS), ROWS)
            for h in range(halves):
                lanes = slice(h * LANES, (h + 1) * LANES)
                rows = row_ref[h, here, :]
                spread = [jnp.broadcast_to(rows[r : r + 1, :], (ROWS, LANES)) for r in range(6)]
                tiles.append((product_ref, lanes, spread))
        for at in range(0, nodes, ROWS):
            here = slice(at, at + ROWS)
            if fresh and start_ref is None:
                totals = [jnp.zeros((ROWS, LANES), jnp.float32)] * 4
            else:
                totals = [(start_ref if fresh else sum_ref)[c, here, :] for c in range(4)]
            for product_ref, lanes, spread in tiles:
                r = lax.rsqrt(jnp.maximum(product_ref[0, here, lanes], 1.0))
                cube = r * (r * r)
                direct = r + cube
                along = product_ref[1, here, lanes] * cube
                for c in range(3):
                    totals[c] = totals[c] + (direct * spread[3 + c] - along * spread[c])
                totals[3] = totals[3] + along
            for c in range(4):
                sum_ref[c, here, :] = totals[c]

    def chunk(first, count):
        multiply(first, product_refs[0:2])
        for i in range(0, count, 4):
            multiply(first + i + 2, product_refs[2:4])
            add(first + i, product_refs[0:2], fresh=i == 0 and not looped)
            if i + 4 < count:
                multiply(first + i + 4, product_refs[0:2])
            add(first + i + 2, product_refs[2:4])

    if not looped:
        chunk(0, blocks)
    else:

        def step(i, _):
            chunk(i * CHUNK, CHUNK)
            return 0

        lax.fori_loop(0, blocks // CHUNK, step, 0)


def velocity_rows(own_ref, info_ref, sum_ref, scale):
    nodes = sum_ref.shape[1]
    sums = []
    for c in range(4):
        parts = [
            jnp.sum(sum_ref[c, at : at + LANES, :].T, axis=0, keepdims=True)
            for at in range(0, nodes, LANES)
        ]
        sums.append(jnp.concatenate(parts, axis=1))
    shift = [info_ref[2 * ROWS + c : 2 * ROWS + c + 1, 0:1] for c in range(3)]
    x = [v - o for v, o in zip(own_rows(own_ref, nodes), shift)]
    return [(sums[c] + x[c] * sums[3]) * (inverse_blob * scale) for c in range(3)]


def membrane(x, neighbours_ref, params_ref):
    nodes = x[0].shape[1]
    force = [[], [], []]
    for at in range(0, nodes, LANES):
        here = slice(at, at + LANES)
        points = [neighbours_ref[0:6, here], neighbours_ref[6:12, here]]
        edges = []
        for index in points:
            local = index & (LANES - 1)
            group = index // LANES
            component = []
            for c in range(3):
                found = jnp.zeros(index.shape, jnp.float32)
                for part in range(nodes // LANES):
                    source = jnp.broadcast_to(x[c][:, part * LANES : (part + 1) * LANES], index.shape)
                    taken = jnp.take_along_axis(source, local, axis=1, mode="promise_in_bounds")
                    found = jnp.where(group == part, taken, found)
                component.append(found - x[c][:, here])
            edges.append(component)
        near, far = edges
        length = params_ref[0:6, here]
        stretch = (near[0] * near[0] + near[1] * near[1] + near[2] * near[2]) / (length * length)
        tension = (stretch - 1.0) / (stretch + 1.0) / length
        for c in range(3):
            surface = jnp.sum(tension * near[c], axis=0, keepdims=True)
            bending = jnp.sum((2.0 / 9.0) * near[c] - (1.0 / 18.0) * far[c], axis=0, keepdims=True)
            bending = bending - params_ref[8 + c : 9 + c, here]
            force[c].append(params_ref[6:7, here] * surface + params_ref[7:8, here] * bending)
    return [jnp.concatenate(parts, axis=1) for parts in force]


def near_kernel(source_ref, own_ref, side_ref, sum_ref, *work):
    pair_sums(source_ref, own_ref, side_ref, None, sum_ref, work)


def advance(scale, sources, work, position_ref, sum_ref, neighbours_ref, params_ref, outs):
    out_ref, moved_ref, next_side_ref = outs
    own_ref, side_ref = sources[1:3]
    velocity = velocity_rows(own_ref, work[4], sum_ref, scale)
    nodes = velocity[0].shape[1]
    x = [position_ref[c : c + 1, :] + time_step * velocity[c] for c in range(3)]
    for c in range(3):
        moved_ref[c : c + 1, :] = x[c]
    scaled = [inverse_blob * v for v in x]
    force = membrane(x, neighbours_ref, params_ref)
    make_left(scaled, select_of(side_ref), next_side_ref, work[4], work[2])
    for chip in range(out_ref.shape[0]):
        for c in range(3):
            out_ref[chip, :, c * nodes : (c + 1) * nodes] = scaled[c]
            out_ref[chip, :, (3 + c) * nodes : (4 + c) * nodes] = force[c]


def first_kernel(scale, capacity, *refs):
    *sources, start_ref, position_ref, neighbours_ref, near_ref, far_ref = refs[:8]
    outs, (params_ref, sum_ref, *work) = refs[8:11], refs[11:]
    pick_slots(capacity, near_ref, far_ref, sources[2], params_ref)
    pair_sums(*sources, start_ref, sum_ref, work)
    advance(scale, sources, work, position_ref, sum_ref, neighbours_ref, params_ref, outs)


def step_kernel(scale, *refs):
    *sources, start_ref, position_ref, neighbours_ref, params_ref = refs[:7]
    outs, (sum_ref, *work) = refs[7:10], refs[10:]
    pair_sums(*sources, start_ref, sum_ref, work)
    advance(scale, sources, work, position_ref, sum_ref, neighbours_ref, params_ref, outs)


def last_kernel(scale, *refs):
    *sources, start_ref, velocity_ref, sum_ref = refs[:6]
    work = refs[6:]
    pair_sums(*sources, start_ref, sum_ref, work)
    velocity = velocity_rows(sources[1], work[4], sum_ref, scale)
    for c in range(3):
        velocity_ref[c : c + 1, :] = velocity[c]


def spread(copies):
    near = lax.all_to_all(copies, CHIPS, split_axis=0, concat_axis=0, tiled=True)
    far = lax.ppermute(near, "core", [(0, 1), (1, 0)])
    return near, far


def call(kernel, out_shape, operands, blocks, nodes, keeps_sums):
    pairs = blocks * nodes * nodes
    sums = [] if keeps_sums else [pltpu.VMEM((4, nodes, LANES), jnp.float32)]
    return pl.pallas_call(
        kernel,
        out_shape=out_shape,
        in_specs=[VMEM] * len(operands),
        out_specs=jax.tree.map(lambda _: VMEM, out_shape),
        scratch_shapes=sums
        + [
            pltpu.VMEM((nodes // LANES, blocks * PIECES, LANES), jnp.float32),
            pltpu.VMEM((nodes // LANES, blocks * ROWS, LANES), jnp.float32),
            pltpu.VMEM((PIECES, nodes), jnp.float32),
            pltpu.VMEM((2 * nodes, DEPTH), jnp.bfloat16),
            pltpu.VMEM((3 * ROWS, LANES), jnp.float32),
        ]
        + [pltpu.VMEM((2, nodes, nodes), jnp.float32)] * 4,
        compiler_params=GRANT,
        cost_estimate=pl.CostEstimate(flops=31 * pairs, bytes_accessed=8 * 3 * nodes * LANES, transcendentals=pairs),
    )(*operands)


def body(positions, forces, neighbours, patch_owner, rest_length, moduli, rest_bend):
    devices = lax.axis_size(AXES)
    nodes = positions.shape[1]
    chips = devices // 2
    scale = 1.0 / math.sqrt(devices * nodes)
    capacity = rest_length.shape[1] // devices
    copies_shape = jax.ShapeDtypeStruct((chips, 1, 6 * nodes), jnp.float32)
    params_shape = jax.ShapeDtypeStruct((PARAMS, nodes), jnp.float32)
    row_shape = jax.ShapeDtypeStruct((3, nodes), jnp.float32)
    step_shapes = (copies_shape, row_shape, side_shape(nodes))
    sums_shape = jax.ShapeDtypeStruct((4, nodes, LANES), jnp.float32)
    select = jnp.asarray(selectors())
    position = positions
    owner = patch_owner.reshape(1, nodes)
    copies, side = pack(
        positions, forces, rest_length, moduli, rest_bend, owner, select, devices
    )
    for step in range(STEPS + 1):
        near, far = spread(copies)
        shared = (copies, side)
        start = call(near_kernel, sums_shape, (near.reshape(-1, LANES),) + shared, chips, nodes, True)
        operands = (far.reshape(-1, LANES),) + shared + (start,)
        if step == 0:
            operands += (position, neighbours, near, far)
            kernel = functools.partial(first_kernel, scale, capacity)
            shapes = (*step_shapes, params_shape)
            copies, position, side, params = call(kernel, shapes, operands, chips, nodes, False)
        elif step < STEPS:
            operands += (position, neighbours, params)
            kernel = functools.partial(step_kernel, scale)
            copies, position, side = call(kernel, step_shapes, operands, chips, nodes, False)
    velocity = call(functools.partial(last_kernel, scale), row_shape, operands, chips, nodes, False)
    return position, velocity


def solution(mesh):
    tgt, src = mesh.devices.shape
    by_core = Mesh(mesh.devices.reshape(tgt, src // 2, 2), AXES)
    placed = (
        P(None, AXES),
        P(None, AXES),
        P(None, AXES),
        P(AXES, None),
        P(None, AXES),
        P(None, AXES),
        P(None, AXES),
    )
    return jax.shard_map(
        body,
        mesh=by_core,
        in_specs=placed,
        out_specs=(P(None, AXES), P(None, AXES)),
        check_vma=False,
    )
```
